768 devices in a mesh: rows: 24 (over z, core), rep: 32 (over y, x).
Axes of the slice: x: 4, y: 8, z: 12, core: 2. Of those that a mesh axis runs over, the one named last changes fastest.
Arguments:
- out_grad: bfloat16 [98304, 256], P(('rows', 'rep')), may hold values from -6 to 6
- pre_relu: bfloat16 [98304, 256], P(('rows', 'rep')), may hold values from -6 to 6
- features: bfloat16 [98304, 256], P('rows'), may hold values from -0.059814453 to 0.059814453
- weight: bfloat16 [256, 256], replicated, may hold values from -0.375 to 0.375
- send_rows: int32 [768, 24, 32], P(('rows', 'rep')), may hold values from 0 to 127
- send_count: int32 [768, 24], P(('rows', 'rep')), may hold values from 1 to 32, as said below
- tile_index: int32 [768, 96], P(('rows', 'rep')), may hold values from 0 to 191, as said below
- tile_count: int32 [768], P(('rows', 'rep')), may hold values from 1 to 96, as said below
- tile_values: bfloat16 [768, 96, 128, 128], P(('rows', 'rep')), may hold values from -0.109375 to 0.109375
Outputs:
- feature_grad: bfloat16 [98304, 256], P(('rows', 'rep'))
- weight_grad: float32 [256, 256], replicated
The draws below stay inside these ranges and needn't reach their ends.
Inputs may be any that keep to these rules, and one draw needn't show every extreme that they name: `send_count`: every device sends exactly 32 rows to at least one peer. `tile_index`: distinct on each device; a position k is row block k // 32 and column block k % 32. `tile_count`: some device has all 96 slots live.
All inputs are finite; a program needn't handle non-finite values.
Results may differ from the reference program's by a relative error of at most 0.0049.
Values may be sent and summed in bfloat16 or wider, within the bound.
No kernel may reach another device: no remote copies, remote signals or barrier semaphores. Data moves between devices by JAX's collectives and lax.ppermute only.
A program may use at most 64 MiB of HBM per device.

```python
import jax
import jax.numpy as jnp
from jax import lax

D = 256
TILE = 128
NODE_DEV = 128
SEND = 32
NODE_R = 4096
NODES = 98304
CB = 32
RB = 6
TILES = 96
N_ROWS = 24
N_REP = 32


def draw_send_count(key, part):
    key = jax.random.fold_in(key, 11)
    first, second = jax.random.split(key)
    lowest = max(1, SEND // 4)
    counts = jax.random.randint(first, (N_ROWS * N_REP, N_ROWS), lowest, SEND + 1)
    chosen = jax.random.randint(second, (N_ROWS * N_REP, 1), 0, N_ROWS)
    columns = jnp.arange(N_ROWS, dtype=jnp.int32)[None, :]
    return jnp.where(columns == chosen, SEND, counts).astype(jnp.int32)


def draw_tile_index(key, part):
    key = jax.random.fold_in(key, 12)
    device_keys = jax.random.split(key, N_ROWS * N_REP)
    return jax.vmap(lambda one_key: jax.random.permutation(one_key, RB * CB)[:TILES])(device_keys).astype(jnp.int32)


def draw_tile_count(key, part):
    key = jax.random.fold_in(key, 13)
    first, second = jax.random.split(key)
    counts = jax.random.randint(first, (N_ROWS * N_REP,), 1, TILES + 1)
    chosen = jax.random.randint(second, (), 0, N_ROWS * N_REP)
    return jnp.where(jnp.arange(N_ROWS * N_REP, dtype=jnp.int32) == chosen, TILES, counts).astype(jnp.int32)


def touch_ends(drawn, key, low, high):
    shape = drawn.shape
    spot = [jax.random.randint(jax.random.fold_in(key, axis), (), 0, shape[axis]) for axis in range(len(shape))]
    drawn = drawn.at[tuple(spot)].set(low)
    longest = shape.index(max(shape))
    spot[longest] = (spot[longest] + 1) % shape[longest]
    return drawn.at[tuple(spot)].set(high)


def levels(key, dims, shards, least, largest):
    loudness = 1.0
    for dim, parts in shards:
        draws = jax.random.uniform(jax.random.fold_in(jax.random.fold_in(key, 6), dim), (parts,), jnp.float32, least / len(shards), largest / len(shards))
        loudness = loudness * jnp.repeat(jnp.exp(draws), dims[dim] // parts).reshape((-1,) + (1,) * (len(dims) - 1 - dim))
    return loudness


def scatter_about(key, extent, spread, most, pieces=(), kind=jnp.bfloat16):
    result = spread * jax.random.normal(key, extent, jnp.float32)
    if pieces:
        result = result * levels(key, extent, pieces, -0.22, 0.18)
    return jnp.clip(result, -most, most).astype(kind)


def setup_inputs(seed: int = 0) -> dict:
    key_of = jax.random.split(jax.random.key(seed), 10)
    return {
        "out_grad": scatter_about(key_of[0], (NODES, D), 1.0, 6.0, ((0, 768),)),
        "pre_relu": scatter_about(key_of[1], (NODES, D), 1.0, 6.0, ((0, 768),)),
        "features": scatter_about(key_of[2], (NODES, D), 0.01, 0.059814453, ((0, 24),)),
        "weight": scatter_about(key_of[3], (D, D), D ** -0.5, 0.375),
        "send_rows": touch_ends(jax.random.randint(key_of[4], (N_ROWS * N_REP, N_ROWS, SEND), 0, NODE_DEV), jax.random.fold_in(key_of[4], 1), 0, NODE_DEV - 1).astype(jnp.int32),
        "send_count": draw_send_count(jax.random.fold_in(key_of[9], 71), 0),
        "tile_index": draw_tile_index(jax.random.fold_in(key_of[9], 71), 0),
        "tile_count": draw_tile_count(jax.random.fold_in(key_of[9], 71), 0),
        "tile_values": scatter_about(key_of[8], (N_ROWS * N_REP, TILES, TILE, TILE), (RB * TILE * N_REP // 8) ** -0.5, 0.109375, ((0, 768),)),
    }


def reference(out_grad, pre_relu, features, weight, send_rows, send_count, tile_index, tile_count, tile_values):
    grad_pre = jnp.where(pre_relu > 0, out_grad, jnp.zeros_like(out_grad))
    peer_iota = jnp.arange(N_ROWS, dtype=jnp.int32)
    slot_iota = jnp.arange(SEND, dtype=jnp.int32)
    tile_iota = jnp.arange(TILES, dtype=jnp.int32)
    pad_count = RB * TILE - N_ROWS * SEND

    def group(group_index):
        def replica_step(total, replica):
            senders = peer_iota * N_REP + replica
            peer_lists = send_rows[senders, group_index]
            peer_counts = send_count[senders, group_index]
            lookup = (senders[:, None] * NODE_DEV + peer_lists).astype(jnp.int32)
            fetched = grad_pre[lookup]
            live = (slot_iota[None, :] < peer_counts[:, None])[:, :, None]
            fetched = jnp.where(live, fetched, jnp.zeros_like(fetched))
            flat_rows = jnp.concatenate([fetched.reshape(N_ROWS * SEND, D), jnp.zeros((pad_count, D), jnp.bfloat16)], axis=0)
            row_blocks = flat_rows.reshape(RB, TILE, D)
            device = group_index * N_REP + replica
            places = tile_index[device]
            kept = (tile_iota < tile_count[device])[:, None, None]
            tiles_now = jnp.where(kept, tile_values[device], jnp.zeros_like(tile_values[device])).astype(jnp.float32)
            picked = row_blocks[places // CB].astype(jnp.float32)
            contrib = jnp.einsum("tkl,tkd->tld", tiles_now, picked)
            total = total.at[places % CB].add(contrib)
            return total, None

        total, _ = lax.scan(replica_step, jnp.zeros((CB, TILE, D), jnp.float32), jnp.arange(N_REP, dtype=jnp.int32))
        return total.reshape(NODE_R, D)

    grads = lax.map(group, jnp.arange(N_ROWS, dtype=jnp.int32)).reshape(NODES, D)
    rounded = grads.astype(jnp.bfloat16)
    feature_grad = lax.dot_general(rounded, weight, (((1,), (1,)), ((), ())), preferred_element_type=jnp.float32).astype(jnp.bfloat16)
    weight_grad = lax.dot_general(features.astype(jnp.float32), grads, (((0,), (0,)), ((), ())), precision=lax.Precision.HIGHEST)
    return feature_grad, weight_grad
```

```python
import jax
import jax.numpy as jnp
from jax import lax
from jax.experimental import pallas as pl
from jax.experimental.pallas import tpu as pltpu
from jax.sharding import PartitionSpec as P


def tile_products(index_ref, count_ref, tiles_ref, rows_ref, features_ref, out_ref, weight_ref, dense, rows_t):
    row_blocks = rows_ref.shape[0] // tiles_ref.shape[1]
    col_blocks = out_ref.shape[0]
    size = tiles_ref.shape[1]
    dense[...] = jnp.zeros_like(dense)

    def place(t, carry):
        k = index_ref[t]
        dense[lax.rem(k, col_blocks) * row_blocks + lax.div(k, col_blocks)] = tiles_ref[t]
        return carry

    lax.fori_loop(0, count_ref[0], place, 0)
    rows_t[...] = rows_ref[...].T
    weight_ref[...] = jnp.zeros_like(weight_ref)

    def columns(j, carry):
        left = dense[pl.ds(2 * j * row_blocks, row_blocks)].reshape(row_blocks * size, size)
        right = dense[pl.ds((2 * j + 1) * row_blocks, row_blocks)].reshape(row_blocks * size, size)
        pair = jnp.concatenate([left, right], axis=1)
        part = jnp.dot(rows_t[...], pair, preferred_element_type=jnp.float32).astype(jnp.bfloat16)
        out_ref[2 * j] = part[:, :size]
        out_ref[2 * j + 1] = part[:, size:]
        weight_ref[...] += jnp.dot(
            part,
            features_ref[pl.ds(pl.multiple_of(2 * j * size, 2 * size), 2 * size), :],
            preferred_element_type=jnp.float32,
        )
        return carry

    lax.fori_loop(0, col_blocks // 2, columns, 0)


def per_device(
    out_grad, pre_relu, features, weight, send_rows, send_count, tile_index, tile_count, tile_values
):
    node_dev, width = out_grad.shape
    n_rows = lax.axis_size("rows")
    n_rep = lax.axis_size("rep")
    per_peer = send_rows.shape[2]
    tile_size = tile_values.shape[2]
    node_group = features.shape[0]
    col_blocks = node_group // tile_size
    total_rows = n_rows * per_peer
    row_blocks = total_rows // tile_size

    grad_pre = jnp.where(pre_relu > 0, out_grad, jnp.zeros_like(out_grad))
    slot_iota = jnp.arange(per_peer, dtype=jnp.int32)
    wanted = jnp.where(slot_iota[None, :] < send_count[0][:, None], send_rows[0], -1)
    picks = (wanted[:, :, None] == jnp.arange(node_dev, dtype=jnp.int32)).astype(jnp.bfloat16)
    outgoing = lax.dot_general(
        picks, grad_pre, (((2,), (0,)), ((), ())), preferred_element_type=jnp.float32
    ).astype(jnp.bfloat16)
    received = lax.all_to_all(outgoing, "rows", split_axis=0, concat_axis=0, tiled=True)

    partial_t, weight_part = pl.pallas_call(
        tile_products,
        out_shape=(
            jax.ShapeDtypeStruct((col_blocks, width, tile_size), jnp.bfloat16),
            jax.ShapeDtypeStruct((width, width), jnp.float32),
        ),
        in_specs=[
            pl.BlockSpec(memory_space=pltpu.SMEM),
            pl.BlockSpec(memory_space=pltpu.SMEM),
            pl.BlockSpec(memory_space=pltpu.VMEM),
            pl.BlockSpec(memory_space=pltpu.VMEM),
            pl.BlockSpec(memory_space=pltpu.VMEM),
        ],
        out_specs=(pl.BlockSpec(memory_space=pltpu.VMEM), pl.BlockSpec(memory_space=pltpu.VMEM)),
        scratch_shapes=[
            pltpu.VMEM((row_blocks * col_blocks, tile_size, tile_size), jnp.bfloat16),
            pltpu.VMEM((width, total_rows), jnp.bfloat16),
        ],
        compiler_params=pltpu.CompilerParams(vmem_limit_bytes=32 * 1024 * 1024),
    )(tile_index[0], tile_count, tile_values[0], received.reshape(total_rows, width), features)

    weight_terms = lax.all_to_all(
        weight_part.reshape(n_rep, width // n_rep, width), "rep", split_axis=0, concat_axis=0, tiled=True
    )
    parts = lax.all_to_all(partial_t, "rep", split_axis=0, concat_axis=0, tiled=True)

    own = jnp.sum(weight_terms, axis=0)
    everyone = lax.all_to_all(
        jnp.broadcast_to(own[None], (n_rows,) + own.shape), "rows", split_axis=0, concat_axis=0, tiled=True
    )
    own = jnp.sum(everyone, axis=0)
    whole = lax.all_to_all(
        jnp.broadcast_to(own[None], (n_rep,) + own.shape), "rep", split_axis=0, concat_axis=0, tiled=True
    )
    weight_grad = whole.reshape(width, width).T

    grads_t = jnp.sum(parts.astype(jnp.float32), axis=0)
    feature_grad = lax.dot_general(
        grads_t.astype(jnp.bfloat16),
        weight,
        (((0,), (1,)), ((), ())),
        preferred_element_type=jnp.float32,
    ).astype(jnp.bfloat16)
    return (feature_grad, weight_grad)


def solution(mesh):
    return jax.shard_map(
        per_device,
        mesh=mesh,
        in_specs=(
            P(("rows", "rep"), None),
            P(("rows", "rep"), None),
            P("rows", None),
            P(),
            P(("rows", "rep"), None, None),
            P(("rows", "rep"), None),
            P(("rows", "rep"), None),
            P(("rows", "rep")),
            P(("rows", "rep"), None, None, None),
        ),
        out_specs=(P(("rows", "rep"), None), P()),
        check_vma=False,
    )
```

```python
import functools

import jax
import jax.numpy as jnp
from jax import lax
from jax.experimental import pallas as pl
from jax.experimental.pallas import tpu as pltpu
from jax.sharding import PartitionSpec as P

STEPS = 8
VMEM_BYTES = 60000000
FINISH_VMEM_BYTES = 16000000
SMEM = pl.BlockSpec(memory_space=pltpu.SMEM)
VMEM = pl.BlockSpec(memory_space=pltpu.VMEM)


def place_tiles(row_blocks, index_ref, count_ref, tiles_ref, features_ref, dense_ref, mixed_ref, total):
    size = tiles_ref.shape[1]
    col_blocks = dense_ref.shape[0] // row_blocks
    dense_ref[...] = jnp.zeros_like(dense_ref)
    total[...] = jnp.zeros_like(total)

    def place(t, carry):
        k = index_ref[t]
        dense_ref[lax.rem(k, col_blocks) * row_blocks + lax.div(k, col_blocks)] = tiles_ref[t]
        return carry

    lax.fori_loop(0, count_ref[0], place, 0)

    def mix(j, carry):
        left = dense_ref[pl.ds(2 * j * row_blocks, row_blocks)].reshape(row_blocks * size, size)
        right = dense_ref[pl.ds((2 * j + 1) * row_blocks, row_blocks)].reshape(row_blocks * size, size)
        total[...] += jnp.dot(
            jnp.concatenate([left, right], axis=1),
            features_ref[pl.ds(pl.multiple_of(2 * j * size, 2 * size), 2 * size), :],
            preferred_element_type=jnp.float32,
        )
        return carry

    lax.fori_loop(0, col_blocks // 2, mix, 0)
    mixed_ref[...] = total[...].astype(mixed_ref.dtype)


def partial_products(low, row_blocks, rows_ref, dense_ref, out_ref, rows_t):
    depth = rows_t.shape[0]
    size = dense_ref.shape[1]

    @pl.when(pl.program_id(0) == 0)
    def _():
        rows_t[...] = rows_ref[:, low : low + depth].T

    for j in range(out_ref.shape[0] // 2):
        left = dense_ref[2 * j * row_blocks : (2 * j + 1) * row_blocks].reshape(row_blocks * size, size)
        right = dense_ref[(2 * j + 1) * row_blocks : (2 * j + 2) * row_blocks].reshape(row_blocks * size, size)
        part = jnp.dot(
            rows_t[...], jnp.concatenate([left, right], axis=1), preferred_element_type=jnp.float32
        ).astype(out_ref.dtype)
        out_ref[2 * j, :depth] = part[:, :size]
        out_ref[2 * j + 1, :depth] = part[:, size:]


def first_products(row_blocks, rows_ref, mixed_ref, dense_ref, out_ref, rows_t, weight_term):
    depth = rows_t.shape[0]
    size = dense_ref.shape[1]
    count = out_ref.shape[0]
    share = weight_term.shape[0] // (count * STEPS)

    @pl.when(pl.program_id(0) == 0)
    def _():
        weight_term[...] = lax.dot_general(
            mixed_ref[...], rows_ref[...], (((0,), (0,)), ((), ())), preferred_element_type=jnp.float32
        )

    partial_products(0, row_blocks, rows_ref, dense_ref, out_ref, rows_t)
    for j in range(count):
        first = pl.multiple_of((pl.program_id(0) * count + j) * share, share)
        own = weight_term[pl.ds(first, share), :]
        out_ref[j, depth:] = jnp.concatenate([own[:, :size], own[:, size:]], axis=0).astype(out_ref.dtype)


def finish(first_ref, second_ref, weight_ref, feature_grad_ref, weight_grad_ref):
    half, size = first_ref.shape
    share = (second_ref.shape[1] - half) // 2
    second = second_ref[0, :half].astype(jnp.float32)
    for p in range(1, second_ref.shape[0]):
        second += second_ref[p, :half].astype(jnp.float32)
    grads_t = jnp.concatenate([first_ref[...], second.astype(jnp.bfloat16)], axis=0)
    feature_grad_ref[...] = lax.dot_general(
        grads_t, weight_ref[...], (((0,), (1,)), ((), ())), preferred_element_type=jnp.float32
    ).astype(feature_grad_ref.dtype)
    for p in range(second_ref.shape[0]):
        own = second_ref[p, half:].astype(jnp.float32)
        weight_grad_ref[p * share : (p + 1) * share] = jnp.concatenate([own[:share], own[share:]], axis=1)


def per_device(
    out_grad, pre_relu, features, weight, send_rows, send_count, tile_index, tile_count, tile_values
):
    node_dev, width = out_grad.shape
    n_rows = lax.axis_size("rows")
    n_rep = lax.axis_size("rep")
    per_peer = send_rows.shape[2]
    size = tile_values.shape[2]
    col_blocks = features.shape[0] // size
    total_rows = n_rows * per_peer
    row_blocks = total_rows // size
    half = width // 2
    share = width // n_rep
    extra = share * width // size
    exchange = functools.partial(lax.all_to_all, split_axis=0, concat_axis=0, tiled=True)

    grad_pre = jnp.where(pre_relu > 0, out_grad, jnp.zeros_like(out_grad))
    slot_iota = jnp.arange(per_peer, dtype=jnp.int32)
    wanted = jnp.where(slot_iota[None, :] < send_count[0][:, None], send_rows[0], -1)
    picks = (wanted[:, :, None] == jnp.arange(node_dev, dtype=jnp.int32)).astype(jnp.bfloat16)
    outgoing = lax.dot_general(
        picks, grad_pre, (((2,), (0,)), ((), ())), preferred_element_type=jnp.float32
    ).astype(jnp.bfloat16)
    received = exchange(outgoing, "rows").reshape(total_rows, width)

    dense, mixed = pl.pallas_call(
        functools.partial(place_tiles, row_blocks),
        out_shape=(
            jax.ShapeDtypeStruct((col_blocks * row_blocks, size, size), jnp.bfloat16),
            jax.ShapeDtypeStruct((total_rows, width), jnp.bfloat16),
        ),
        in_specs=[SMEM, SMEM, VMEM, VMEM],
        out_specs=(VMEM, VMEM),
        scratch_shapes=[pltpu.VMEM((total_rows, width), jnp.float32)],
        compiler_params=pltpu.CompilerParams(vmem_limit_bytes=VMEM_BYTES),
        cost_estimate=pl.CostEstimate(flops=1600000000, bytes_accessed=24000000, transcendentals=0),
    )(tile_index[0], tile_count, tile_values[0], features)

    rows_spec = pl.BlockSpec((total_rows, width), lambda i: (0, 0))
    dense_spec = pl.BlockSpec((col_blocks // STEPS * row_blocks, size, size), lambda i: (i, 0, 0))
    out_spec = pl.BlockSpec((col_blocks // STEPS, half + extra, size), lambda i: (i, 0, 0))
    out_shape = jax.ShapeDtypeStruct((col_blocks, half + extra, size), jnp.bfloat16)
    rows_t = pltpu.VMEM((half, total_rows), jnp.bfloat16)
    params = pltpu.CompilerParams(vmem_limit_bytes=VMEM_BYTES)
    first = pl.pallas_call(
        functools.partial(first_products, row_blocks),
        grid=(STEPS,),
        out_shape=out_shape,
        in_specs=[rows_spec, rows_spec, dense_spec],
        out_specs=out_spec,
        scratch_shapes=[rows_t, pltpu.VMEM((width, width), jnp.float32)],
        compiler_params=params,
        cost_estimate=pl.CostEstimate(flops=900000000, bytes_accessed=8000000, transcendentals=0),
    )(received, mixed, dense)
    first = exchange(first, "rep")

    second = pl.pallas_call(
        functools.partial(partial_products, half, row_blocks),
        grid=(STEPS,),
        out_shape=out_shape,
        in_specs=[rows_spec, dense_spec],
        out_specs=out_spec,
        scratch_shapes=[rows_t],
        compiler_params=params,
        cost_estimate=pl.CostEstimate(flops=800000000, bytes_accessed=8000000, transcendentals=0),
    )(received, dense)

    own = jnp.sum(first[:, half:].astype(jnp.float32), axis=0)
    own = jnp.sum(exchange(jnp.broadcast_to(own[None], (n_rows, extra, size)), "rows"), axis=0)
    own = jnp.broadcast_to(own.astype(jnp.bfloat16)[None], (n_rep, extra, size))
    second = exchange(second.at[:, half:].set(own), "rep")
    first = jnp.sum(first[:, :half].astype(jnp.float32), axis=0).astype(jnp.bfloat16)
    return pl.pallas_call(
        finish,
        out_shape=(
            jax.ShapeDtypeStruct((node_dev, width), jnp.bfloat16),
            jax.ShapeDtypeStruct((width, width), jnp.float32),
        ),
        in_specs=[VMEM, VMEM, VMEM],
        out_specs=(VMEM, VMEM),
        compiler_params=pltpu.CompilerParams(vmem_limit_bytes=FINISH_VMEM_BYTES),
    )(first, second, weight)


def solution(mesh):
    return jax.shard_map(
        per_device,
        mesh=mesh,
        in_specs=(
            P(("rows", "rep"), None),
            P(("rows", "rep"), None),
            P("rows", None),
            P(),
            P(("rows", "rep"), None, None),
            P(("rows", "rep"), None),
            P(("rows", "rep"), None),
            P(("rows", "rep")),
            P(("rows", "rep"), None, None, None),
        ),
        out_specs=(P(("rows", "rep"), None), P()),
        check_vma=False,
    )
```

```python
import functools

import jax
import jax.numpy as jnp
from jax import lax
from jax.experimental import pallas as pl
from jax.experimental.pallas import tpu as pltpu
from jax.sharding import PartitionSpec as P

STEPS = 8
VMEM_BYTES = 60000000
FINISH_VMEM_BYTES = 16000000
SMEM = pl.BlockSpec(memory_space=pltpu.SMEM)
VMEM = pl.BlockSpec(memory_space=pltpu.VMEM)


def place_tiles(index_ref, count_ref, tiles_ref, features_ref, turned_ref, mixed_ref, dense, total):
    col_blocks, row_blocks, size, _ = dense.shape
    dense[...] = jnp.zeros_like(dense)
    turned_ref[...] = jnp.zeros_like(turned_ref)
    total[...] = jnp.zeros_like(total)
    count = count_ref[0]

    def place(t, carry):
        k = index_ref[t]
        c, r = lax.rem(k, col_blocks), lax.div(k, col_blocks)
        tile = jnp.where(t < count, tiles_ref[t], jnp.zeros_like(tiles_ref[t]))
        dense[c, r] = tile
        first = pl.multiple_of(c * size, size)
        turned_ref[pl.ds(first, size), pl.ds(pl.multiple_of(r * size, size), size)] = tile.T
        return carry

    lax.fori_loop(0, tiles_ref.shape[0], place, 0, unroll=4)

    def mix(j, carry):
        left = dense[2 * j].reshape(row_blocks * size, size)
        right = dense[2 * j + 1].reshape(row_blocks * size, size)
        total[...] += jnp.dot(
            jnp.concatenate([left, right], axis=1),
            features_ref[pl.ds(pl.multiple_of(2 * j * size, 2 * size), 2 * size), :],
            preferred_element_type=jnp.float32,
        )
        return carry

    lax.fori_loop(0, col_blocks // 2, mix, 0)
    mixed_ref[...] = total[...].astype(mixed_ref.dtype).T


def lanes_to_rows(block, size):
    return jnp.concatenate([block[:, i : i + size] for i in range(0, block.shape[1], size)], axis=0)


def rows_to_lanes(block, count):
    rows = block.shape[0] // count
    return jnp.concatenate([block[i * rows : (i + 1) * rows] for i in range(count)], axis=1)


def products(bounds, rows_ref, mixed_ref, turned_ref, *refs):
    *outs, weight_term = refs
    count = outs[0].shape[0]
    size = outs[0].shape[2]
    share = weight_term.shape[0] // (count * STEPS)

    @pl.when(pl.program_id(0) == 0)
    def _():
        weight_term[...] = jnp.dot(mixed_ref[...], rows_ref[...], preferred_element_type=jnp.float32)

    part = jnp.dot(turned_ref[...], rows_ref[...], preferred_element_type=jnp.float32).astype(outs[0].dtype)
    for j in range(count):
        for out, (low, high) in zip(outs, bounds):
            block = lanes_to_rows(part[j * size + low : j * size + high], size)
            out[j, : block.shape[0]] = block
        first = pl.multiple_of((pl.program_id(0) * count + j) * share, share)
        own = lanes_to_rows(weight_term[pl.ds(first, share), :], size)
        outs[0][j, outs[0].shape[1] - own.shape[0] :] = own.astype(outs[0].dtype)


def finish(lanes, sums_ref, middle_ref, last_ref, weight_ref, feature_grad_ref, weight_grad_ref):
    share = weight_grad_ref.shape[0] // last_ref.shape[0]
    rows = last_ref.shape[1] - share * lanes
    last = last_ref[0, :rows].astype(jnp.float32)
    for p in range(1, last_ref.shape[0]):
        last += last_ref[p, :rows].astype(jnp.float32)
    grads = jnp.concatenate(
        [rows_to_lanes(block, lanes) for block in (sums_ref[...], middle_ref[...], last.astype(jnp.bfloat16))], axis=0
    )
    feature_grad_ref[...] = lax.dot_general(
        grads, weight_ref[...], (((1,), (1,)), ((), ())), preferred_element_type=jnp.float32
    ).astype(feature_grad_ref.dtype)
    for p in range(last_ref.shape[0]):
        own = last_ref[p, rows:].astype(jnp.float32)
        weight_grad_ref[p * share : (p + 1) * share] = rows_to_lanes(own, lanes)


def sum_over_rows(term):
    n = lax.axis_size("rows")

    def shifted(value, to):
        return lax.ppermute(value, "rows", [(i, to(i)) for i in range(n)])

    term = term + shifted(term, lambda i: i ^ 1)
    term = term + shifted(term, lambda i: i ^ 2)
    third = n // 3
    up, down = shifted(term, lambda i: (i + third) % n), shifted(term, lambda i: (i - third) % n)
    place = lax.axis_index("rows") // third
    a = jnp.where(place == 0, term, jnp.where(place == 1, up, down))
    b = jnp.where(place == 1, term, jnp.where(place == 2, up, down))
    c = jnp.where(place == 2, term, jnp.where(place == 0, up, down))
    term = (a + b) + c
    return term + shifted(term, lambda i: (i + n // 2) % n)


def per_device(
    out_grad, pre_relu, features, weight, send_rows, send_count, tile_index, tile_count, tile_values
):
    node_dev, width = out_grad.shape
    n_rows = lax.axis_size("rows")
    n_rep = lax.axis_size("rep")
    per_peer = send_rows.shape[2]
    size = tile_values.shape[2]
    col_blocks = features.shape[0] // size
    total_rows = n_rows * per_peer
    row_blocks = total_rows // size
    lanes = width // size
    share = width // n_rep
    extra = share * lanes
    cuts = (0, size // 4, 3 * size // 4, size)
    bounds = tuple(zip(cuts[:-1], cuts[1:]))
    exchange = functools.partial(lax.all_to_all, split_axis=0, concat_axis=0, tiled=True)

    grad_pre = jnp.where(pre_relu > 0, out_grad, jnp.zeros_like(out_grad))
    slot_iota = jnp.arange(per_peer, dtype=jnp.int32)
    wanted = jnp.where(slot_iota[None, :] < send_count[0][:, None], send_rows[0], -1)
    picks = (wanted[:, :, None] == jnp.arange(node_dev, dtype=jnp.int32)).astype(jnp.bfloat16)
    outgoing = lax.dot_general(
        picks, grad_pre, (((2,), (0,)), ((), ())), preferred_element_type=jnp.float32
    ).astype(jnp.bfloat16)
    received = exchange(outgoing, "rows").reshape(total_rows, width)

    turned, mixed = pl.pallas_call(
        place_tiles,
        out_shape=(
            jax.ShapeDtypeStruct((col_blocks * size, total_rows), jnp.bfloat16),
            jax.ShapeDtypeStruct((width, total_rows), jnp.bfloat16),
        ),
        in_specs=[SMEM, SMEM, VMEM, VMEM],
        out_specs=(VMEM, VMEM),
        scratch_shapes=[
            pltpu.VMEM((col_blocks, row_blocks, size, size), jnp.bfloat16),
            pltpu.VMEM((total_rows, width), jnp.float32),
        ],
        compiler_params=pltpu.CompilerParams(vmem_limit_bytes=VMEM_BYTES),
        cost_estimate=pl.CostEstimate(flops=1600000000, bytes_accessed=24000000, transcendentals=0),
    )(tile_index[0], tile_count, tile_values[0], features)

    depths = [(high - low) * lanes + more for (low, high), more in zip(bounds, (extra, 0, extra))]
    first, middle, last = pl.pallas_call(
        functools.partial(products, bounds),
        grid=(STEPS,),
        out_shape=tuple(jax.ShapeDtypeStruct((col_blocks, depth, size), jnp.bfloat16) for depth in depths),
        in_specs=[
            pl.BlockSpec((total_rows, width), lambda i: (0, 0)),
            pl.BlockSpec((width, total_rows), lambda i: (0, 0)),
            pl.BlockSpec((col_blocks * size // STEPS, total_rows), lambda i: (i, 0)),
        ],
        out_specs=tuple(pl.BlockSpec((col_blocks // STEPS, depth, size), lambda i: (i, 0, 0)) for depth in depths),
        scratch_shapes=[pltpu.VMEM((width, width), jnp.float32)],
        compiler_params=pltpu.CompilerParams(vmem_limit_bytes=VMEM_BYTES),
        cost_estimate=pl.CostEstimate(flops=1700000000, bytes_accessed=9000000, transcendentals=0),
    )(received, mixed, turned)

    first = exchange(first, "rep")
    middle = exchange(middle, "rep")
    own = sum_over_rows(jnp.sum(first[:, depths[0] - extra :].astype(jnp.float32), axis=0))
    own = jnp.broadcast_to(own.astype(jnp.bfloat16)[None], (n_rep, extra, size))
    last = exchange(last.at[:, depths[2] - extra :].set(own), "rep")
    sums = [
        jnp.sum(part.astype(jnp.float32), axis=0).astype(jnp.bfloat16)
        for part in (first[:, : depths[0] - extra], middle)
    ]
    return pl.pallas_call(
        functools.partial(finish, lanes),
        out_shape=(
            jax.ShapeDtypeStruct((node_dev, width), jnp.bfloat16),
            jax.ShapeDtypeStruct((width, width), jnp.float32),
        ),
        in_specs=[VMEM, VMEM, VMEM, VMEM],
        out_specs=(VMEM, VMEM),
        compiler_params=pltpu.CompilerParams(vmem_limit_bytes=FINISH_VMEM_BYTES),
    )(sums[0], sums[1], last, weight)


def solution(mesh):
    return jax.shard_map(
        per_device,
        mesh=mesh,
        in_specs=(
            P(("rows", "rep"), None),
            P(("rows", "rep"), None),
            P("rows", None),
            P(),
            P(("rows", "rep"), None, None),
            P(("rows", "rep"), None),
            P(("rows", "rep"), None),
            P(("rows", "rep")),
            P(("rows", "rep"), None, None, None),
        ),
        out_specs=(P(("rows", "rep"), None), P()),
        check_vma=False,
    )
```

```python
import functools

import jax
import jax.numpy as jnp
from jax import lax
from jax.experimental import pallas as pl
from jax.experimental.pallas import tpu as pltpu
from jax.sharding import PartitionSpec as P

VMEM_BYTES = 24000000
SMEM = pl.BlockSpec(memory_space=pltpu.SMEM)
VMEM = pl.BlockSpec(memory_space=pltpu.VMEM)
HBM = pl.BlockSpec(memory_space=pltpu.HBM)


def place_tiles(index_ref, count_ref, tiles_ref, features_ref, turned_ref, mixed_ref, dense, turned, total, sem):
    col_blocks, row_blocks, size, _ = dense.shape
    dense[...] = jnp.zeros_like(dense)
    turned[...] = jnp.zeros_like(turned)
    total[...] = jnp.zeros_like(total)
    count = count_ref[0]

    def place(t, carry):
        k = index_ref[t]
        c, r = lax.rem(k, col_blocks), lax.div(k, col_blocks)
        tile = jnp.where(t < count, tiles_ref[t], jnp.zeros_like(tiles_ref[t]))
        dense[c, r] = tile
        first = pl.multiple_of(c * size, size)
        turned[pl.ds(first, size), pl.ds(pl.multiple_of(r * size, size), size)] = tile.T
        return carry

    lax.fori_loop(0, tiles_ref.shape[0], place, 0, unroll=4)
    copy = pltpu.make_async_copy(turned, turned_ref, sem)
    copy.start()

    def mix(j, carry):
        left = dense[2 * j].reshape(row_blocks * size, size)
        right = dense[2 * j + 1].reshape(row_blocks * size, size)
        total[...] += jnp.dot(
            jnp.concatenate([left, right], axis=1),
            features_ref[pl.ds(pl.multiple_of(2 * j * size, 2 * size), 2 * size), :],
            preferred_element_type=jnp.float32,
        )
        return carry

    lax.fori_loop(0, col_blocks // 2, mix, 0)
    mixed_ref[...] = total[...].astype(mixed_ref.dtype).T
    copy.wait()


def weight_terms(mixed_ref, rows_ref, out_ref):
    depth, width = out_ref.shape[1:]
    slices = mixed_ref.shape[0] // depth
    term = jnp.dot(mixed_ref[...], rows_ref[...], preferred_element_type=jnp.float32)
    out_ref[:slices] = term.reshape(slices, depth, width)
    out_ref[slices:] = jnp.zeros((out_ref.shape[0] - slices, depth, width), jnp.float32)


def products(odd_ref, rows_ref, turned_ref, keep_ref, near_ref, far_ref, turned, sems):
    blocks, size, _ = keep_ref.shape
    half = size // 2
    odd = odd_ref[0]

    def fetch(g):
        span = pl.ds(pl.multiple_of(2 * g * size, 2 * size), 2 * size)
        return pltpu.make_async_copy(turned_ref.at[span], turned.at[span], sems.at[g])

    def start(g, carry):
        fetch(g).start()
        return carry

    def pair(g, carry):
        fetch(g).wait()
        kept = turned[pl.ds(pl.multiple_of((2 * g + odd) * size, size), size), :]
        sent = turned[pl.ds(pl.multiple_of((2 * g + 1 - odd) * size, size), size), :]
        part = jnp.dot(
            jnp.concatenate([kept, sent], axis=0), rows_ref[...], preferred_element_type=jnp.float32
        )
        keep_ref[g] = part[:size]
        near_ref[g] = part[size : size + half].astype(near_ref.dtype)
        far_ref[g] = part[size + half :].astype(far_ref.dtype)
        return carry

    lax.fori_loop(0, blocks, start, 0)
    lax.fori_loop(0, blocks, pair, 0)


def add_partners(keep_ref, near_ref, far_ref, share_ref, out_ref):
    blocks, size, _ = keep_ref.shape
    half = size // 2
    share = share_ref[...].astype(out_ref.dtype)

    def block(g, carry):
        out_ref[g, :half] = (keep_ref[g, :half] + near_ref[g].astype(jnp.float32)).astype(out_ref.dtype)
        out_ref[g, half:size] = (keep_ref[g, half:] + far_ref[g].astype(jnp.float32)).astype(out_ref.dtype)
        out_ref[g, size:] = share
        return carry

    lax.fori_loop(0, blocks, block, 0)


def per_device(
    out_grad, pre_relu, features, weight, send_rows, send_count, tile_index, tile_count, tile_values
):
    node_dev, width = out_grad.shape
    n_rows = lax.axis_size("rows")
    n_rep = lax.axis_size("rep")
    per_peer = send_rows.shape[2]
    size = tile_values.shape[2]
    col_blocks = features.shape[0] // size
    total_rows = n_rows * per_peer
    row_blocks = total_rows // size
    slices = 16
    depth = width // slices
    blocks = col_blocks // 2
    groups = [list(range(odd, n_rep, 2)) for odd in (0, 1)]
    exchange = functools.partial(lax.all_to_all, split_axis=0, concat_axis=0, tiled=True)
    params = pltpu.CompilerParams(vmem_limit_bytes=VMEM_BYTES)

    def swapped(value, mask):
        return lax.ppermute(value, "rep", [(i, i ^ mask) for i in range(n_rep)])

    grad_pre = jnp.where(pre_relu > 0, out_grad, jnp.zeros_like(out_grad))
    slot_iota = jnp.arange(per_peer, dtype=jnp.int32)
    wanted = jnp.where(slot_iota[None, :] < send_count[0][:, None], send_rows[0], -1)
    picks = (wanted[:, :, None] == jnp.arange(node_dev, dtype=jnp.int32)).astype(jnp.bfloat16)
    outgoing = lax.dot_general(
        picks, grad_pre, (((2,), (0,)), ((), ())), preferred_element_type=jnp.float32
    ).astype(jnp.bfloat16)
    received = exchange(outgoing, "rows").reshape(total_rows, width)

    turned, mixed = pl.pallas_call(
        place_tiles,
        out_shape=(
            pltpu.HBM((col_blocks * size, total_rows), jnp.bfloat16),
            jax.ShapeDtypeStruct((width, total_rows), jnp.bfloat16),
        ),
        in_specs=[SMEM, SMEM, VMEM, VMEM],
        out_specs=(HBM, VMEM),
        scratch_shapes=[
            pltpu.VMEM((col_blocks, row_blocks, size, size), jnp.bfloat16),
            pltpu.VMEM((col_blocks * size, total_rows), jnp.bfloat16),
            pltpu.VMEM((total_rows, width), jnp.float32),
            pltpu.SemaphoreType.DMA,
        ],
        compiler_params=params,
        cost_estimate=pl.CostEstimate(flops=1600000000, bytes_accessed=24000000, transcendentals=0),
    )(tile_index[0], tile_count, tile_values[0], features)

    term = pl.pallas_call(
        weight_terms,
        out_shape=jax.ShapeDtypeStruct((n_rows, depth, width), jnp.float32),
        in_specs=[VMEM, VMEM],
        out_specs=VMEM,
        compiler_params=params,
    )(mixed, received)
    share = jnp.sum(exchange(term, "rows"), axis=0)
    share = share + swapped(share, 1)

    odd = (lax.axis_index("rep") % 2).astype(jnp.int32)[None]
    half = jax.ShapeDtypeStruct((blocks, size // 2, width), jnp.bfloat16)
    keep, near, far = pl.pallas_call(
        products,
        out_shape=(jax.ShapeDtypeStruct((blocks, size, width), jnp.float32), half, half),
        in_specs=[SMEM, VMEM, HBM],
        out_specs=(VMEM, VMEM, VMEM),
        scratch_shapes=[
            pltpu.VMEM((col_blocks * size, total_rows), jnp.bfloat16),
            pltpu.SemaphoreType.DMA((blocks,)),
        ],
        compiler_params=params,
        cost_estimate=pl.CostEstimate(flops=1700000000, bytes_accessed=9000000, transcendentals=0),
    )(odd, received, pltpu.with_memory_space_constraint(turned, pltpu.HBM))
    near, far = swapped(near, 1), swapped(far, 3)

    parts = pl.pallas_call(
        add_partners,
        out_shape=jax.ShapeDtypeStruct((blocks, size + depth, width), jnp.bfloat16),
        in_specs=[VMEM, VMEM, VMEM, VMEM],
        out_specs=VMEM,
        compiler_params=params,
    )(keep, near, far, share)
    parts = exchange(parts, "rep", axis_index_groups=groups)

    own = jnp.sum(parts[:, size:].astype(jnp.float32), axis=0).astype(jnp.bfloat16)
    whole = exchange(jnp.broadcast_to(own[None], (n_rows, depth, width)), "rows")
    weight_grad = whole[:slices].reshape(width, width).astype(jnp.float32)

    grads = jnp.sum(parts[:, :size].astype(jnp.float32), axis=0)
    feature_grad = lax.dot_general(
        grads.astype(jnp.bfloat16),
        weight,
        (((1,), (1,)), ((), ())),
        preferred_element_type=jnp.float32,
    ).astype(jnp.bfloat16)
    return (feature_grad, weight_grad)


def solution(mesh):
    return jax.shard_map(
        per_device,
        mesh=mesh,
        in_specs=(
            P(("rows", "rep"), None),
            P(("rows", "rep"), None),
            P("rows", None),
            P(),
            P(("rows", "rep"), None, None),
            P(("rows", "rep"), None),
            P(("rows", "rep"), None),
            P(("rows", "rep")),
            P(("rows", "rep"), None, None, None),
        ),
        out_specs=(P(("rows", "rep"), None), P()),
        check_vma=False,
    )
```

```python
import functools

import jax
import jax.numpy as jnp
from jax import lax
from jax.experimental import pallas as pl
from jax.experimental.pallas import tpu as pltpu
from jax.sharding import PartitionSpec as P

VMEM_BYTES = 24000000
SLICES = 8
PAIRS = 4
SMEM = pl.BlockSpec(memory_space=pltpu.SMEM)
VMEM = pl.BlockSpec(memory_space=pltpu.VMEM)
HBM = pl.BlockSpec(memory_space=pltpu.HBM)


def place_tiles(index_ref, count_ref, tiles_ref, features_ref, turned_ref, mixed_ref, dense, turned, total, sem):
    col_blocks, row_blocks, size, _ = dense.shape
    dense[...] = jnp.zeros_like(dense)
    turned[...] = jnp.zeros_like(turned)
    total[...] = jnp.zeros_like(total)
    count = count_ref[0]

    def place(t, carry):
        k = index_ref[t]
        c, r = lax.rem(k, col_blocks), lax.div(k, col_blocks)
        tile = jnp.where(t < count, tiles_ref[t], jnp.zeros_like(tiles_ref[t]))
        dense[c, r] = tile
        first = pl.multiple_of(c * size, size)
        turned[pl.ds(first, size), pl.ds(pl.multiple_of(r * size, size), size)] = tile.T
        return carry

    lax.fori_loop(0, tiles_ref.shape[0], place, 0, unroll=4)
    copy = pltpu.make_async_copy(turned, turned_ref, sem)
    copy.start()

    def mix(j, carry):
        left = dense[2 * j].reshape(row_blocks * size, size)
        right = dense[2 * j + 1].reshape(row_blocks * size, size)
        total[...] += jnp.dot(
            jnp.concatenate([left, right], axis=1),
            features_ref[pl.ds(pl.multiple_of(2 * j * size, 2 * size), 2 * size), :],
            preferred_element_type=jnp.float32,
        )
        return carry

    lax.fori_loop(0, col_blocks // 2, mix, 0)
    mixed_ref[...] = total[...].astype(mixed_ref.dtype).T
    copy.wait()


def weight_terms(mixed_ref, rows_ref, out_ref):
    depth, width = out_ref.shape[1:]
    slices = mixed_ref.shape[0] // depth
    term = jnp.dot(mixed_ref[...], rows_ref[...], preferred_element_type=jnp.float32)
    term = term.astype(out_ref.dtype).reshape(slices, depth, width)
    for first in range(0, out_ref.shape[0], slices):
        out_ref[first : first + slices] = term


def spread_sum(terms_ref, after_ref, out_ref):
    del after_ref
    total = terms_ref[0].astype(jnp.float32)
    for i in range(1, terms_ref.shape[0]):
        total += terms_ref[i].astype(jnp.float32)
    total = total.astype(out_ref.dtype)
    for p in range(out_ref.shape[0]):
        out_ref[p] = total


def products(odd_ref, rows_ref, turned_ref, keep_ref, near_ref, far_ref, turned, sems):
    blocks, size, _ = keep_ref.shape
    half = size // 2
    odd = odd_ref[0]
    copies = []
    for g in range(blocks):
        span = pl.ds(2 * g * size, 2 * size)
        copies.append(pltpu.make_async_copy(turned_ref.at[span], turned.at[span], sems.at[g]))
        copies[-1].start()
    for first in range(0, blocks, PAIRS):
        taken = []
        for g in range(first, first + PAIRS):
            copies[g].wait()
            for c in (2 * g + odd, 2 * g + 1 - odd):
                taken.append(turned[pl.ds(pl.multiple_of(c * size, size), size), :])
        part = jnp.dot(jnp.concatenate(taken, axis=0), rows_ref[...], preferred_element_type=jnp.float32)
        for i in range(PAIRS):
            kept, sent = part[2 * i * size : (2 * i + 1) * size], part[(2 * i + 1) * size : (2 * i + 2) * size]
            keep_ref[first + i] = kept
            near_ref[first + i] = sent[:half].astype(near_ref.dtype)
            far_ref[first + i] = sent[half:].astype(far_ref.dtype)


def add_partners(keep_ref, near_ref, far_ref, out_ref):
    blocks, size, _ = keep_ref.shape
    half = size // 2

    def block(g, carry):
        out_ref[g, :half] = (keep_ref[g, :half] + near_ref[g].astype(jnp.float32)).astype(out_ref.dtype)
        out_ref[g, half:size] = (keep_ref[g, half:] + far_ref[g].astype(jnp.float32)).astype(out_ref.dtype)
        return carry

    lax.fori_loop(0, blocks, block, 0, unroll=2)


def put_in_order(place_ref, own_ref, one_ref, two_ref, four_ref, out_ref):
    depth = own_ref.shape[0]
    pieces = [own_ref[...], one_ref[...]]
    pieces += [two_ref[i * depth : (i + 1) * depth] for i in range(2)]
    pieces += [four_ref[i * depth : (i + 1) * depth] for i in range(4)]
    for j, piece in enumerate(pieces):
        first = pl.multiple_of((place_ref[0] ^ j) * depth, depth)
        out_ref[pl.ds(first, depth), :] = piece


def per_device(
    out_grad, pre_relu, features, weight, send_rows, send_count, tile_index, tile_count, tile_values
):
    node_dev, width = out_grad.shape
    n_rows = lax.axis_size("rows")
    n_rep = lax.axis_size("rep")
    per_peer = send_rows.shape[2]
    size = tile_values.shape[2]
    col_blocks = features.shape[0] // size
    total_rows = n_rows * per_peer
    row_blocks = total_rows // size
    depth = width // SLICES
    blocks = col_blocks // 2
    groups = [list(range(odd, n_rep, 2)) for odd in (0, 1)]
    exchange = functools.partial(lax.all_to_all, split_axis=0, concat_axis=0, tiled=True)
    params = pltpu.CompilerParams(vmem_limit_bytes=VMEM_BYTES)

    def swapped(value, mask, axis="rep"):
        return lax.ppermute(value, axis, [(i, i ^ mask) for i in range(lax.axis_size(axis))])

    grad_pre = jnp.where(pre_relu > 0, out_grad, jnp.zeros_like(out_grad))
    slot_iota = jnp.arange(per_peer, dtype=jnp.int32)
    wanted = jnp.where(slot_iota[None, :] < send_count[0][:, None], send_rows[0], -1)
    picks = (wanted[:, :, None] == jnp.arange(node_dev, dtype=jnp.int32)).astype(jnp.bfloat16)
    outgoing = lax.dot_general(
        picks, grad_pre, (((2,), (0,)), ((), ())), preferred_element_type=jnp.float32
    ).astype(jnp.bfloat16)
    received = exchange(outgoing, "rows").reshape(total_rows, width)

    turned, mixed = pl.pallas_call(
        place_tiles,
        out_shape=(
            pltpu.HBM((col_blocks * size, total_rows), jnp.bfloat16),
            jax.ShapeDtypeStruct((width, total_rows), jnp.bfloat16),
        ),
        in_specs=[SMEM, SMEM, VMEM, VMEM],
        out_specs=(HBM, VMEM),
        scratch_shapes=[
            pltpu.VMEM((col_blocks, row_blocks, size, size), jnp.bfloat16),
            pltpu.VMEM((col_blocks * size, total_rows), jnp.bfloat16),
            pltpu.VMEM((total_rows, width), jnp.float32),
            pltpu.SemaphoreType.DMA,
        ],
        compiler_params=params,
        cost_estimate=pl.CostEstimate(flops=1600000000, bytes_accessed=24000000, transcendentals=0),
    )(tile_index[0], tile_count, tile_values[0], features)

    term = pl.pallas_call(
        weight_terms,
        out_shape=jax.ShapeDtypeStruct((n_rows, depth, width), jnp.bfloat16),
        in_specs=[VMEM, VMEM],
        out_specs=VMEM,
        compiler_params=params,
    )(mixed, received)
    terms = exchange(term, "rows")

    odd = (lax.axis_index("rep") % 2).astype(jnp.int32)[None]
    half = jax.ShapeDtypeStruct((blocks, size // 2, width), jnp.bfloat16)
    keep, near, far = pl.pallas_call(
        products,
        out_shape=(jax.ShapeDtypeStruct((blocks, size, width), jnp.float32), half, half),
        in_specs=[SMEM, VMEM, HBM],
        out_specs=(VMEM, VMEM, VMEM),
        scratch_shapes=[
            pltpu.VMEM((col_blocks * size, total_rows), jnp.bfloat16),
            pltpu.SemaphoreType.DMA((blocks,)),
        ],
        compiler_params=params,
        cost_estimate=pl.CostEstimate(flops=1700000000, bytes_accessed=9000000, transcendentals=0),
    )(odd, received, pltpu.with_memory_space_constraint(turned, pltpu.HBM))
    share = pl.pallas_call(
        spread_sum,
        out_shape=jax.ShapeDtypeStruct((n_rep, depth, width), jnp.bfloat16),
        in_specs=[VMEM, pl.BlockSpec(memory_space=pl.ANY)],
        out_specs=VMEM,
        compiler_params=params,
    )(terms, near)
    own = jnp.sum(exchange(share, "rep").astype(jnp.float32), axis=0)
    near, far = swapped(near, 1), swapped(far, 3)

    parts = pl.pallas_call(
        add_partners,
        out_shape=jax.ShapeDtypeStruct((blocks, size, width), jnp.bfloat16),
        in_specs=[VMEM, VMEM, VMEM],
        out_specs=VMEM,
        compiler_params=params,
    )(keep, near, far)
    parts = exchange(parts, "rep", axis_index_groups=groups)

    one = swapped(own, 1, "rows")
    two = swapped(jnp.concatenate([own, one], axis=0), 2, "rows")
    four = swapped(jnp.concatenate([own, one, two], axis=0), 4, "rows")
    weight_grad = pl.pallas_call(
        put_in_order,
        out_shape=jax.ShapeDtypeStruct((width, width), jnp.float32),
        in_specs=[SMEM, VMEM, VMEM, VMEM, VMEM],
        out_specs=VMEM,
        compiler_params=params,
    )((lax.axis_index("rows") % SLICES).astype(jnp.int32)[None], own, one, two, four)

    grads = jnp.sum(parts.astype(jnp.float32), axis=0)
    feature_grad = lax.dot_general(
        grads.astype(jnp.bfloat16),
        weight,
        (((1,), (1,)), ((), ())),
        preferred_element_type=jnp.float32,
    ).astype(jnp.bfloat16)
    return (feature_grad, weight_grad)


def solution(mesh):
    return jax.shard_map(
        per_device,
        mesh=mesh,
        in_specs=(
            P(("rows", "rep"), None),
            P(("rows", "rep"), None),
            P("rows", None),
            P(),
            P(("rows", "rep"), None, None),
            P(("rows", "rep"), None),
            P(("rows", "rep"), None),
            P(("rows", "rep")),
            P(("rows", "rep"), None, None, None),
        ),
        out_specs=(P(("rows", "rep"), None), P()),
        check_vma=False,
    )
```

```python
import functools

import jax
import jax.numpy as jnp
from jax import lax
from jax.experimental import pallas as pl
from jax.experimental.pallas import tpu as pltpu
from jax.sharding import PartitionSpec as P

VMEM_BYTES = 24000000
SLICES = 8
RING = 4
GROUPS = 2
SMEM = pl.BlockSpec(memory_space=pltpu.SMEM)
VMEM = pl.BlockSpec(memory_space=pltpu.VMEM)
HBM = pl.BlockSpec(memory_space=pltpu.HBM)


def place_tiles(index_ref, count_ref, tiles_ref, features_ref, turned_ref, mixed_ref, dense, turned, total, sem):
    col_blocks, row_blocks, size, _ = dense.shape
    dense[...] = jnp.zeros_like(dense)
    turned[...] = jnp.zeros_like(turned)
    total[...] = jnp.zeros_like(total)
    count = count_ref[0]

    def place(t, carry):
        k = index_ref[t]
        c, r = lax.rem(k, col_blocks), lax.div(k, col_blocks)
        tile = jnp.where(t < count, tiles_ref[t], jnp.zeros_like(tiles_ref[t]))
        dense[c, r] = tile
        first = pl.multiple_of(c * size, size)
        turned[pl.ds(first, size), pl.ds(pl.multiple_of(r * size, size), size)] = tile.T
        return carry

    lax.fori_loop(0, tiles_ref.shape[0], place, 0, unroll=4)
    copy = pltpu.make_async_copy(turned, turned_ref, sem)
    copy.start()

    def mix(j, carry):
        left = dense[2 * j].reshape(row_blocks * size, size)
        right = dense[2 * j + 1].reshape(row_blocks * size, size)
        total[...] += jnp.dot(
            jnp.concatenate([left, right], axis=1),
            features_ref[pl.ds(pl.multiple_of(2 * j * size, 2 * size), 2 * size), :],
            preferred_element_type=jnp.float32,
        )
        return carry

    lax.fori_loop(0, col_blocks // 2, mix, 0)
    mixed_ref[...] = total[...].astype(mixed_ref.dtype).T
    copy.wait()


def weight_terms(mixed_ref, rows_ref, out_ref):
    depth, width = out_ref.shape[1:]
    slices = mixed_ref.shape[0] // depth
    term = jnp.dot(mixed_ref[...], rows_ref[...], preferred_element_type=jnp.float32)
    term = term.astype(out_ref.dtype).reshape(slices, depth, width)
    for first in range(0, out_ref.shape[0], slices):
        out_ref[first : first + slices] = term


def spread_sum(terms_ref, after_ref, out_ref):
    del after_ref
    total = terms_ref[0].astype(jnp.float32)
    for i in range(1, terms_ref.shape[0]):
        total += terms_ref[i].astype(jnp.float32)
    total = total.astype(out_ref.dtype)
    for p in range(out_ref.shape[0]):
        out_ref[p] = total


def products(place_ref, rows_ref, turned_ref, keep_ref, up_ref, down_ref, next_ref, last_ref, turned, sems):
    groups, size, _ = keep_ref.shape
    half = size // 2
    place = place_ref[0]
    copies = []
    for g in range(groups):
        span = pl.ds(RING * g * size, RING * size)
        copies.append(pltpu.make_async_copy(turned_ref.at[span], turned.at[span], sems.at[g]))
        copies[-1].start()
    for first in range(0, groups, GROUPS):
        taken = []
        for g in range(first, first + GROUPS):
            copies[g].wait()
            for ahead in range(RING):
                c = RING * g + ((place + ahead) & (RING - 1))
                taken.append(turned[pl.ds(pl.multiple_of(c * size, size), size), :])
        part = jnp.dot(jnp.concatenate(taken, axis=0), rows_ref[...], preferred_element_type=jnp.float32)
        for i in range(GROUPS):
            own, one, two, three = [part[(RING * i + j) * size : (RING * i + j + 1) * size] for j in range(RING)]
            g = first + i
            keep_ref[g] = own
            up_ref[g] = two[:half].astype(up_ref.dtype)
            up_ref[groups + g] = one[half:].astype(up_ref.dtype)
            down_ref[g] = two[half:].astype(down_ref.dtype)
            down_ref[groups + g] = three[:half].astype(down_ref.dtype)
            next_ref[g] = one[:half]
            last_ref[g] = three[half:]


def relay(next_ref, last_ref, up_ref, down_ref, next_out_ref, last_out_ref):
    groups = next_ref.shape[0]
    for g in range(groups):
        next_out_ref[g] = (next_ref[g] + up_ref[g].astype(jnp.float32)).astype(next_out_ref.dtype)
        last_out_ref[g] = (last_ref[g] + down_ref[g].astype(jnp.float32)).astype(last_out_ref.dtype)


def add_ring(keep_ref, up_ref, down_ref, next_ref, last_ref, out_ref):
    groups, size, _ = keep_ref.shape
    half = size // 2
    for g in range(groups):
        low = keep_ref[g, :half] + down_ref[groups + g].astype(jnp.float32) + next_ref[g].astype(jnp.float32)
        high = keep_ref[g, half:] + up_ref[groups + g].astype(jnp.float32) + last_ref[g].astype(jnp.float32)
        out_ref[g, :half] = low.astype(out_ref.dtype)
        out_ref[g, half:] = high.astype(out_ref.dtype)


def put_in_order(place_ref, own_ref, one_ref, two_ref, four_ref, out_ref):
    depth = own_ref.shape[0]
    pieces = [own_ref[...], one_ref[...]]
    pieces += [two_ref[i * depth : (i + 1) * depth] for i in range(2)]
    pieces += [four_ref[i * depth : (i + 1) * depth] for i in range(4)]
    for j, piece in enumerate(pieces):
        first = pl.multiple_of((place_ref[0] ^ j) * depth, depth)
        out_ref[pl.ds(first, depth), :] = piece


def per_device(
    out_grad, pre_relu, features, weight, send_rows, send_count, tile_index, tile_count, tile_values
):
    node_dev, width = out_grad.shape
    n_rows = lax.axis_size("rows")
    n_rep = lax.axis_size("rep")
    per_peer = send_rows.shape[2]
    size = tile_values.shape[2]
    col_blocks = features.shape[0] // size
    total_rows = n_rows * per_peer
    row_blocks = total_rows // size
    depth = width // SLICES
    columns = col_blocks // RING
    groups = [list(range(x, n_rep, RING)) for x in range(RING)]
    exchange = functools.partial(lax.all_to_all, split_axis=0, concat_axis=0, tiled=True)
    params = pltpu.CompilerParams(vmem_limit_bytes=VMEM_BYTES)

    def swapped(value, mask, axis="rep"):
        return lax.ppermute(value, axis, [(i, i ^ mask) for i in range(lax.axis_size(axis))])

    def passed(value, step):
        return lax.ppermute(value, "rep", [(i, i - i % RING + (i + step) % RING) for i in range(n_rep)])

    grad_pre = jnp.where(pre_relu > 0, out_grad, jnp.zeros_like(out_grad))
    slot_iota = jnp.arange(per_peer, dtype=jnp.int32)
    wanted = jnp.where(slot_iota[None, :] < send_count[0][:, None], send_rows[0], -1)
    picks = (wanted[:, :, None] == jnp.arange(node_dev, dtype=jnp.int32)).astype(jnp.bfloat16)
    outgoing = lax.dot_general(
        picks, grad_pre, (((2,), (0,)), ((), ())), preferred_element_type=jnp.float32
    ).astype(jnp.bfloat16)
    received = exchange(outgoing, "rows").reshape(total_rows, width)

    turned, mixed = pl.pallas_call(
        place_tiles,
        out_shape=(
            pltpu.HBM((col_blocks * size, total_rows), jnp.bfloat16),
            jax.ShapeDtypeStruct((width, total_rows), jnp.bfloat16),
        ),
        in_specs=[SMEM, SMEM, VMEM, VMEM],
        out_specs=(HBM, VMEM),
        scratch_shapes=[
            pltpu.VMEM((col_blocks, row_blocks, size, size), jnp.bfloat16),
            pltpu.VMEM((col_blocks * size, total_rows), jnp.bfloat16),
            pltpu.VMEM((total_rows, width), jnp.float32),
            pltpu.SemaphoreType.DMA,
        ],
        compiler_params=params,
        cost_estimate=pl.CostEstimate(flops=1600000000, bytes_accessed=24000000, transcendentals=0),
    )(tile_index[0], tile_count, tile_values[0], features)

    term = pl.pallas_call(
        weight_terms,
        out_shape=jax.ShapeDtypeStruct((n_rows, depth, width), jnp.bfloat16),
        in_specs=[VMEM, VMEM],
        out_specs=VMEM,
        compiler_params=params,
    )(mixed, received)
    terms = exchange(term, "rows")

    place = (lax.axis_index("rep") % RING).astype(jnp.int32)[None]
    full = jax.ShapeDtypeStruct((columns, size, width), jnp.float32)
    half = jax.ShapeDtypeStruct((columns, size // 2, width), jnp.float32)
    half_out = jax.ShapeDtypeStruct((columns, size // 2, width), jnp.bfloat16)
    sent = jax.ShapeDtypeStruct((2 * columns, size // 2, width), jnp.bfloat16)
    keep, up, down, ahead, behind = pl.pallas_call(
        products,
        out_shape=(full, sent, sent, half, half),
        in_specs=[SMEM, VMEM, HBM],
        out_specs=(VMEM,) * 5,
        scratch_shapes=[
            pltpu.VMEM((col_blocks * size, total_rows), jnp.bfloat16),
            pltpu.SemaphoreType.DMA((columns,)),
        ],
        compiler_params=params,
        cost_estimate=pl.CostEstimate(flops=1700000000, bytes_accessed=9000000, transcendentals=0),
    )(place, received, pltpu.with_memory_space_constraint(turned, pltpu.HBM))
    up, down = passed(up, 1), passed(down, -1)
    ahead, behind = pl.pallas_call(
        relay,
        out_shape=(half_out, half_out),
        in_specs=[VMEM] * 4,
        out_specs=(VMEM, VMEM),
        compiler_params=params,
    )(ahead, behind, up, down)
    share = pl.pallas_call(
        spread_sum,
        out_shape=jax.ShapeDtypeStruct((n_rep, depth, width), jnp.bfloat16),
        in_specs=[VMEM, pl.BlockSpec(memory_space=pl.ANY)],
        out_specs=VMEM,
        compiler_params=params,
    )(terms, ahead)
    own = jnp.sum(exchange(share, "rep").astype(jnp.float32), axis=0)
    ahead, behind = passed(ahead, 1), passed(behind, -1)
    parts = pl.pallas_call(
        add_ring,
        out_shape=jax.ShapeDtypeStruct((columns, size, width), jnp.bfloat16),
        in_specs=[VMEM] * 5,
        out_specs=VMEM,
        compiler_params=params,
    )(keep, up, down, ahead, behind)
    parts = exchange(parts, "rep", axis_index_groups=groups)

    one = swapped(own, 1, "rows")
    two = swapped(jnp.concatenate([own, one], axis=0), 2, "rows")
    four = swapped(jnp.concatenate([own, one, two], axis=0), 4, "rows")
    weight_grad = pl.pallas_call(
        put_in_order,
        out_shape=jax.ShapeDtypeStruct((width, width), jnp.float32),
        in_specs=[SMEM, VMEM, VMEM, VMEM, VMEM],
        out_specs=VMEM,
        compiler_params=params,
    )((lax.axis_index("rows") % SLICES).astype(jnp.int32)[None], own, one, two, four)

    grads = jnp.sum(parts.astype(jnp.float32), axis=0)
    feature_grad = lax.dot_general(
        grads.astype(jnp.bfloat16),
        weight,
        (((1,), (1,)), ((), ())),
        preferred_element_type=jnp.float32,
    ).astype(jnp.bfloat16)
    return (feature_grad, weight_grad)


def solution(mesh):
    return jax.shard_map(
        per_device,
        mesh=mesh,
        in_specs=(
            P(("rows", "rep"), None),
            P(("rows", "rep"), None),
            P("rows", None),
            P(),
            P(("rows", "rep"), None, None),
            P(("rows", "rep"), None),
            P(("rows", "rep"), None),
            P(("rows", "rep")),
            P(("rows", "rep"), None, None, None),
        ),
        out_specs=(P(("rows", "rep"), None), P()),
        check_vma=False,
    )
```

```python
import functools

import jax
import jax.numpy as jnp
from jax import lax
from jax.experimental import pallas as pl
from jax.experimental.pallas import tpu as pltpu
from jax.sharding import PartitionSpec as P

VMEM_BYTES = 24000000
PICK_VMEM_BYTES = 60000000
SLICES = 8
RING = 4
GROUPS = 2
SMEM = pl.BlockSpec(memory_space=pltpu.SMEM)
VMEM = pl.BlockSpec(memory_space=pltpu.VMEM)
HBM = pl.BlockSpec(memory_space=pltpu.HBM)


def pick_rows(count_ref, out_grad_ref, pre_relu_ref, send_rows_ref, out_ref):
    peers, slots = send_rows_ref.shape
    nodes = out_grad_ref.shape[0]
    grad_pre = jnp.where(pre_relu_ref[...] > 0, out_grad_ref[...], jnp.zeros_like(out_grad_ref))
    slot = lax.broadcasted_iota(jnp.int32, (1, slots), 1)
    node = lax.broadcasted_iota(jnp.int32, (nodes, nodes), 0)
    together = nodes // slots
    for first in range(0, peers, together):
        wanted = [
            jnp.where(slot < count_ref[q], send_rows_ref[q : q + 1, :], -1) for q in range(first, first + together)
        ]
        picks = jnp.where(node == jnp.concatenate(wanted, axis=1), 1.0, 0.0).astype(jnp.bfloat16)
        out_ref[first * slots : (first + together) * slots] = lax.dot_general(
            picks, grad_pre, (((0,), (0,)), ((), ())), preferred_element_type=jnp.float32
        ).astype(out_ref.dtype)


def place_tiles(index_ref, count_ref, tiles_ref, features_ref, turned_ref, mixed_ref, dense, turned, total, sem):
    col_blocks, row_blocks, size, _ = dense.shape
    dense[...] = jnp.zeros_like(dense)
    turned[...] = jnp.zeros_like(turned)
    total[...] = jnp.zeros_like(total)
    count = count_ref[0]

    def place(t, carry):
        k = index_ref[t]
        c, r = lax.rem(k, col_blocks), lax.div(k, col_blocks)
        tile = jnp.where(t < count, tiles_ref[t], jnp.zeros_like(tiles_ref[t]))
        dense[c, r] = tile
        first = pl.multiple_of(c * size, size)
        turned[pl.ds(first, size), pl.ds(pl.multiple_of(r * size, size), size)] = tile.T
        return carry

    lax.fori_loop(0, tiles_ref.shape[0], place, 0, unroll=4)
    copy = pltpu.make_async_copy(turned, turned_ref, sem)
    copy.start()

    def mix(j, carry):
        left = dense[2 * j].reshape(row_blocks * size, size)
        right = dense[2 * j + 1].reshape(row_blocks * size, size)
        total[...] += jnp.dot(
            jnp.concatenate([left, right], axis=1),
            features_ref[pl.ds(pl.multiple_of(2 * j * size, 2 * size), 2 * size), :],
            preferred_element_type=jnp.float32,
        )
        return carry

    lax.fori_loop(0, col_blocks // 2, mix, 0)
    mixed_ref[...] = total[...].astype(mixed_ref.dtype).T
    copy.wait()


def weight_terms(mixed_ref, rows_ref, out_ref):
    depth, width = out_ref.shape[1:]
    slices = mixed_ref.shape[0] // depth
    term = jnp.dot(mixed_ref[...], rows_ref[...], preferred_element_type=jnp.float32)
    term = term.astype(out_ref.dtype).reshape(slices, depth, width)
    for first in range(0, out_ref.shape[0], slices):
        out_ref[first : first + slices] = term


def spread_sum(terms_ref, after_ref, out_ref):
    del after_ref
    total = terms_ref[0].astype(jnp.float32)
    for i in range(1, terms_ref.shape[0]):
        total += terms_ref[i].astype(jnp.float32)
    total = total.astype(out_ref.dtype)
    for p in range(out_ref.shape[0]):
        out_ref[p] = total


def products(
    place_ref, rows_ref, turned_ref, keep_ref, up_ref, down_ref, up_two_ref, down_two_ref, next_ref, last_ref, turned, sems
):
    groups, size, _ = keep_ref.shape
    half = size // 2
    place = place_ref[0]
    copies = []
    for g in range(groups):
        span = pl.ds(RING * g * size, RING * size)
        copies.append(pltpu.make_async_copy(turned_ref.at[span], turned.at[span], sems.at[g]))
        copies[-1].start()
    for first in range(0, groups, GROUPS):
        taken = []
        for g in range(first, first + GROUPS):
            copies[g].wait()
            for ahead in range(RING):
                c = RING * g + ((place + ahead) & (RING - 1))
                taken.append(turned[pl.ds(pl.multiple_of(c * size, size), size), :])
        part = jnp.dot(jnp.concatenate(taken, axis=0), rows_ref[...], preferred_element_type=jnp.float32)
        for i in range(GROUPS):
            own, one, two, three = [part[(RING * i + j) * size : (RING * i + j + 1) * size] for j in range(RING)]
            g = first + i
            keep_ref[g] = own
            up_two_ref[g] = two[:half].astype(up_ref.dtype)
            up_ref[g] = one[half:].astype(up_ref.dtype)
            down_two_ref[g] = two[half:].astype(down_ref.dtype)
            down_ref[g] = three[:half].astype(down_ref.dtype)
            next_ref[g] = one[:half]
            last_ref[g] = three[half:]


def relay(next_ref, last_ref, up_ref, down_ref, next_out_ref, last_out_ref):
    groups = next_ref.shape[0]
    for g in range(groups):
        next_out_ref[g] = (next_ref[g] + up_ref[g].astype(jnp.float32)).astype(next_out_ref.dtype)
        last_out_ref[g] = (last_ref[g] + down_ref[g].astype(jnp.float32)).astype(last_out_ref.dtype)


def add_ring(keep_ref, up_ref, down_ref, next_ref, last_ref, out_ref):
    groups, size, _ = keep_ref.shape
    half = size // 2
    for g in range(groups):
        low = keep_ref[g, :half] + down_ref[g].astype(jnp.float32) + next_ref[g].astype(jnp.float32)
        high = keep_ref[g, half:] + up_ref[g].astype(jnp.float32) + last_ref[g].astype(jnp.float32)
        out_ref[g, :half] = low.astype(out_ref.dtype)
        out_ref[g, half:] = high.astype(out_ref.dtype)


def finish(place_ref, parts_ref, weight_ref, own_ref, one_ref, two_ref, four_ref, feature_grad_ref, weight_grad_ref):
    grads = parts_ref[0].astype(jnp.float32)
    for y in range(1, parts_ref.shape[0]):
        grads += parts_ref[y].astype(jnp.float32)
    feature_grad_ref[...] = lax.dot_general(
        grads.astype(jnp.bfloat16), weight_ref[...], (((1,), (1,)), ((), ())), preferred_element_type=jnp.float32
    ).astype(feature_grad_ref.dtype)
    depth = own_ref.shape[0]
    pieces = [own_ref[...], one_ref[...]]
    pieces += [two_ref[i * depth : (i + 1) * depth] for i in range(2)]
    pieces += [four_ref[i * depth : (i + 1) * depth] for i in range(4)]
    for j, piece in enumerate(pieces):
        first = pl.multiple_of((place_ref[0] ^ j) * depth, depth)
        weight_grad_ref[pl.ds(first, depth), :] = piece


def per_device(
    out_grad, pre_relu, features, weight, send_rows, send_count, tile_index, tile_count, tile_values
):
    node_dev, width = out_grad.shape
    n_rows = lax.axis_size("rows")
    n_rep = lax.axis_size("rep")
    per_peer = send_rows.shape[2]
    size = tile_values.shape[2]
    col_blocks = features.shape[0] // size
    total_rows = n_rows * per_peer
    row_blocks = total_rows // size
    depth = width // SLICES
    columns = col_blocks // RING
    groups = [list(range(x, n_rep, RING)) for x in range(RING)]
    exchange = functools.partial(lax.all_to_all, split_axis=0, concat_axis=0, tiled=True)
    params = pltpu.CompilerParams(vmem_limit_bytes=VMEM_BYTES)

    def swapped(value, mask, axis="rep"):
        return lax.ppermute(value, axis, [(i, i ^ mask) for i in range(lax.axis_size(axis))])

    def passed(value, step):
        return lax.ppermute(value, "rep", [(i, i - i % RING + (i + step) % RING) for i in range(n_rep)])

    outgoing = pl.pallas_call(
        pick_rows,
        out_shape=jax.ShapeDtypeStruct((total_rows, width), jnp.bfloat16),
        in_specs=[SMEM, VMEM, VMEM, VMEM],
        out_specs=VMEM,
        compiler_params=pltpu.CompilerParams(vmem_limit_bytes=PICK_VMEM_BYTES),
    )(send_count[0], out_grad, pre_relu, send_rows[0])
    received = exchange(outgoing.reshape(n_rows, per_peer, width), "rows").reshape(total_rows, width)

    turned, mixed = pl.pallas_call(
        place_tiles,
        out_shape=(
            pltpu.HBM((col_blocks * size, total_rows), jnp.bfloat16),
            jax.ShapeDtypeStruct((width, total_rows), jnp.bfloat16),
        ),
        in_specs=[SMEM, SMEM, VMEM, VMEM],
        out_specs=(HBM, VMEM),
        scratch_shapes=[
            pltpu.VMEM((col_blocks, row_blocks, size, size), jnp.bfloat16),
            pltpu.VMEM((col_blocks * size, total_rows), jnp.bfloat16),
            pltpu.VMEM((total_rows, width), jnp.float32),
            pltpu.SemaphoreType.DMA,
        ],
        compiler_params=params,
        cost_estimate=pl.CostEstimate(flops=1600000000, bytes_accessed=24000000, transcendentals=0),
    )(tile_index[0], tile_count, tile_values[0], features)

    term = pl.pallas_call(
        weight_terms,
        out_shape=jax.ShapeDtypeStruct((n_rows, depth, width), jnp.bfloat16),
        in_specs=[VMEM, VMEM],
        out_specs=VMEM,
        compiler_params=params,
    )(mixed, received)
    terms = exchange(term, "rows")

    place = (lax.axis_index("rep") % RING).astype(jnp.int32)[None]
    full = jax.ShapeDtypeStruct((columns, size, width), jnp.float32)
    half = jax.ShapeDtypeStruct((columns, size // 2, width), jnp.float32)
    half_out = jax.ShapeDtypeStruct((columns, size // 2, width), jnp.bfloat16)
    keep, up, down, up_two, down_two, ahead, behind = pl.pallas_call(
        products,
        out_shape=(full, half_out, half_out, half_out, half_out, half, half),
        in_specs=[SMEM, VMEM, HBM],
        out_specs=(VMEM,) * 7,
        scratch_shapes=[
            pltpu.VMEM((col_blocks * size, total_rows), jnp.bfloat16),
            pltpu.SemaphoreType.DMA((columns,)),
        ],
        compiler_params=params,
        cost_estimate=pl.CostEstimate(flops=1700000000, bytes_accessed=9000000, transcendentals=0),
    )(place, received, pltpu.with_memory_space_constraint(turned, pltpu.HBM))
    up_two, down_two = passed(up_two, 1), passed(down_two, -1)
    ahead, behind = pl.pallas_call(
        relay,
        out_shape=(half_out, half_out),
        in_specs=[VMEM] * 4,
        out_specs=(VMEM, VMEM),
        compiler_params=params,
    )(ahead, behind, up_two, down_two)
    share = pl.pallas_call(
        spread_sum,
        out_shape=jax.ShapeDtypeStruct((n_rep, depth, width), jnp.bfloat16),
        in_specs=[VMEM, pl.BlockSpec(memory_space=pl.ANY)],
        out_specs=VMEM,
        compiler_params=params,
    )(terms, ahead)
    own = jnp.sum(exchange(share, "rep").astype(jnp.float32), axis=0)
    ahead, behind = passed(ahead, 1), passed(behind, -1)
    up, down = passed(up, 1), passed(down, -1)
    parts = pl.pallas_call(
        add_ring,
        out_shape=jax.ShapeDtypeStruct((columns, size, width), jnp.bfloat16),
        in_specs=[VMEM] * 5,
        out_specs=VMEM,
        compiler_params=params,
    )(keep, up, down, ahead, behind)
    parts = exchange(parts, "rep", axis_index_groups=groups)

    one = swapped(own, 1, "rows")
    two = swapped(jnp.concatenate([own, one], axis=0), 2, "rows")
    four = swapped(jnp.concatenate([own, one, two], axis=0), 4, "rows")
    return pl.pallas_call(
        finish,
        out_shape=(
            jax.ShapeDtypeStruct((node_dev, width), jnp.bfloat16),
            jax.ShapeDtypeStruct((width, width), jnp.float32),
        ),
        in_specs=[SMEM] + [VMEM] * 6,
        out_specs=(VMEM, VMEM),
        compiler_params=params,
    )((lax.axis_index("rows") % SLICES).astype(jnp.int32)[None], parts, weight, own, one, two, four)


def solution(mesh):
    return jax.shard_map(
        per_device,
        mesh=mesh,
        in_specs=(
            P(("rows", "rep"), None),
            P(("rows", "rep"), None),
            P("rows", None),
            P(),
            P(("rows", "rep"), None, None),
            P(("rows", "rep"), None),
            P(("rows", "rep"), None),
            P(("rows", "rep")),
            P(("rows", "rep"), None, None, None),
        ),
        out_specs=(P(("rows", "rep"), None), P()),
        check_vma=False,
    )
```

```python
import functools

import jax
import jax.numpy as jnp
from jax import lax
from jax.experimental import pallas as pl
from jax.experimental.pallas import tpu as pltpu
from jax.sharding import PartitionSpec as P

VMEM_BYTES = 24000000
PICK_VMEM_BYTES = 60000000
SLICES = 8
RING = 4
GROUPS = 2
SMEM = pl.BlockSpec(memory_space=pltpu.SMEM)
VMEM = pl.BlockSpec(memory_space=pltpu.VMEM)
HBM = pl.BlockSpec(memory_space=pltpu.HBM)


def pick_rows(count_ref, out_grad_ref, pre_relu_ref, send_rows_ref, out_ref):
    peers, slots = send_rows_ref.shape
    nodes = out_grad_ref.shape[0]
    grad_pre = jnp.where(pre_relu_ref[...] > 0, out_grad_ref[...], jnp.zeros_like(out_grad_ref))
    slot = lax.broadcasted_iota(jnp.int32, (1, slots), 1)
    node = lax.broadcasted_iota(jnp.int32, (nodes, nodes), 0)
    together = nodes // slots
    for first in range(0, peers, together):
        wanted = [
            jnp.where(slot < count_ref[q], send_rows_ref[q : q + 1, :], -1) for q in range(first, first + together)
        ]
        picks = jnp.where(node == jnp.concatenate(wanted, axis=1), 1.0, 0.0).astype(jnp.bfloat16)
        out_ref[first * slots : (first + together) * slots] = lax.dot_general(
            picks, grad_pre, (((0,), (0,)), ((), ())), preferred_element_type=jnp.float32
        ).astype(out_ref.dtype)


def place_tiles(index_ref, count_ref, tiles_ref, features_ref, turned_ref, mixed_ref, dense, turned, total, sem):
    col_blocks, row_blocks, size, _ = dense.shape
    dense[...] = jnp.zeros_like(dense)
    turned[...] = jnp.zeros_like(turned)
    total[...] = jnp.zeros_like(total)
    count = count_ref[0]

    def place(t, carry):
        k = index_ref[t]
        c, r = lax.rem(k, col_blocks), lax.div(k, col_blocks)
        tile = jnp.where(t < count, tiles_ref[t], jnp.zeros_like(tiles_ref[t]))
        dense[c, r] = tile
        first = pl.multiple_of(c * size, size)
        turned[pl.ds(first, size), pl.ds(pl.multiple_of(r * size, size), size)] = tile.T
        return carry

    lax.fori_loop(0, tiles_ref.shape[0], place, 0, unroll=4)
    copy = pltpu.make_async_copy(turned, turned_ref, sem)
    copy.start()

    def mix(j, carry):
        left = dense[2 * j].reshape(row_blocks * size, size)
        right = dense[2 * j + 1].reshape(row_blocks * size, size)
        total[...] += jnp.dot(
            jnp.concatenate([left, right], axis=1),
            features_ref[pl.ds(pl.multiple_of(2 * j * size, 2 * size), 2 * size), :],
            preferred_element_type=jnp.float32,
        )
        return carry

    lax.fori_loop(0, col_blocks // 2, mix, 0)
    mixed_ref[...] = total[...].astype(mixed_ref.dtype).T
    copy.wait()


def weight_terms(mixed_ref, rows_ref, out_ref):
    depth, width = out_ref.shape[1:]
    slices = mixed_ref.shape[0] // depth
    term = jnp.dot(mixed_ref[...], rows_ref[...], preferred_element_type=jnp.float32)
    term = term.astype(out_ref.dtype).reshape(slices, depth, width)
    for first in range(0, out_ref.shape[0], slices):
        out_ref[first : first + slices] = term


def spread_sum(terms_ref, after_ref, out_ref):
    del after_ref
    total = terms_ref[0].astype(jnp.float32)
    for i in range(1, terms_ref.shape[0]):
        total += terms_ref[i].astype(jnp.float32)
    total = total.astype(out_ref.dtype)
    for p in range(out_ref.shape[0]):
        out_ref[p] = total


def products(place_ref, rows_ref, turned_ref, keep_ref, up_ref, down_ref, next_ref, last_ref, turned, sems):
    groups, size, _ = keep_ref.shape
    half = size // 2
    place = place_ref[0]
    copies = []
    for g in range(groups):
        span = pl.ds(RING * g * size, RING * size)
        copies.append(pltpu.make_async_copy(turned_ref.at[span], turned.at[span], sems.at[g]))
        copies[-1].start()
    for first in range(0, groups, GROUPS):
        taken = []
        for g in range(first, first + GROUPS):
            copies[g].wait()
            for ahead in range(RING):
                c = RING * g + ((place + ahead) & (RING - 1))
                taken.append(turned[pl.ds(pl.multiple_of(c * size, size), size), :])
        part = jnp.dot(jnp.concatenate(taken, axis=0), rows_ref[...], preferred_element_type=jnp.float32)
        for i in range(GROUPS):
            own, one, two, three = [part[(RING * i + j) * size : (RING * i + j + 1) * size] for j in range(RING)]
            g = first + i
            keep_ref[g] = own
            up_ref[g] = two[:half].astype(up_ref.dtype)
            down_ref[g] = two[half:].astype(down_ref.dtype)
            next_ref[g] = one[:half]
            last_ref[g] = three[half:]
            if g < groups // 2:
                up_ref[groups + g] = one[half:].astype(up_ref.dtype)
                down_ref[groups + g] = three[:half].astype(down_ref.dtype)
            else:
                next_ref[groups // 2 + g] = one[half:]
                last_ref[groups // 2 + g] = three[:half]


def relay(groups, next_ref, last_ref, up_ref, down_ref, next_out_ref, last_out_ref):
    for g in range(groups):
        next_out_ref[g] = (next_ref[g] + up_ref[g].astype(jnp.float32)).astype(next_out_ref.dtype)
        last_out_ref[g] = (last_ref[g] + down_ref[g].astype(jnp.float32)).astype(last_out_ref.dtype)
    for g in range(groups, next_ref.shape[0]):
        next_out_ref[g] = next_ref[g].astype(next_out_ref.dtype)
        last_out_ref[g] = last_ref[g].astype(last_out_ref.dtype)


def add_ring(keep_ref, up_ref, down_ref, next_ref, last_ref, out_ref):
    groups, size, _ = keep_ref.shape
    half = size // 2
    for g in range(groups):
        if g < groups // 2:
            from_last, from_next = up_ref[groups + g], down_ref[groups + g]
        else:
            from_last, from_next = next_ref[groups // 2 + g], last_ref[groups // 2 + g]
        low = keep_ref[g, :half] + from_next.astype(jnp.float32) + next_ref[g].astype(jnp.float32)
        high = keep_ref[g, half:] + from_last.astype(jnp.float32) + last_ref[g].astype(jnp.float32)
        out_ref[g, :half] = low.astype(out_ref.dtype)
        out_ref[g, half:] = high.astype(out_ref.dtype)


def finish(place_ref, parts_ref, weight_ref, pair_ref, two_ref, four_ref, six_ref, feature_grad_ref, weight_grad_ref):
    grads = parts_ref[0].astype(jnp.float32)
    for y in range(1, parts_ref.shape[0]):
        grads += parts_ref[y].astype(jnp.float32)
    feature_grad_ref[...] = lax.dot_general(
        grads.astype(jnp.bfloat16), weight_ref[...], (((1,), (1,)), ((), ())), preferred_element_type=jnp.float32
    ).astype(feature_grad_ref.dtype)
    depth = pair_ref.shape[0] // 2
    for j in range(SLICES):
        piece_ref = (pair_ref, two_ref, four_ref, six_ref)[j // 2]
        first = pl.multiple_of((place_ref[0] ^ j) * depth, depth)
        piece = piece_ref[(j % 2) * depth : (j % 2 + 1) * depth]
        weight_grad_ref[pl.ds(first, depth), :] = piece.astype(weight_grad_ref.dtype)


def per_device(
    out_grad, pre_relu, features, weight, send_rows, send_count, tile_index, tile_count, tile_values
):
    node_dev, width = out_grad.shape
    n_rows = lax.axis_size("rows")
    n_rep = lax.axis_size("rep")
    per_peer = send_rows.shape[2]
    size = tile_values.shape[2]
    col_blocks = features.shape[0] // size
    total_rows = n_rows * per_peer
    row_blocks = total_rows // size
    depth = width // SLICES
    columns = col_blocks // RING
    groups = [list(range(x, n_rep, RING)) for x in range(RING)]
    exchange = functools.partial(lax.all_to_all, split_axis=0, concat_axis=0, tiled=True)
    params = pltpu.CompilerParams(vmem_limit_bytes=VMEM_BYTES)

    def swapped(value, mask, axis="rep"):
        return lax.ppermute(value, axis, [(i, i ^ mask) for i in range(lax.axis_size(axis))])

    def passed(value, step):
        return lax.ppermute(value, "rep", [(i, i - i % RING + (i + step) % RING) for i in range(n_rep)])

    outgoing = pl.pallas_call(
        pick_rows,
        out_shape=jax.ShapeDtypeStruct((total_rows, width), jnp.bfloat16),
        in_specs=[SMEM, VMEM, VMEM, VMEM],
        out_specs=VMEM,
        compiler_params=pltpu.CompilerParams(vmem_limit_bytes=PICK_VMEM_BYTES),
    )(send_count[0], out_grad, pre_relu, send_rows[0])
    received = exchange(outgoing.reshape(n_rows, per_peer, width), "rows").reshape(total_rows, width)

    turned, mixed = pl.pallas_call(
        place_tiles,
        out_shape=(
            pltpu.HBM((col_blocks * size, total_rows), jnp.bfloat16),
            jax.ShapeDtypeStruct((width, total_rows), jnp.bfloat16),
        ),
        in_specs=[SMEM, SMEM, VMEM, VMEM],
        out_specs=(HBM, VMEM),
        scratch_shapes=[
            pltpu.VMEM((col_blocks, row_blocks, size, size), jnp.bfloat16),
            pltpu.VMEM((col_blocks * size, total_rows), jnp.bfloat16),
            pltpu.VMEM((total_rows, width), jnp.float32),
            pltpu.SemaphoreType.DMA,
        ],
        compiler_params=params,
        cost_estimate=pl.CostEstimate(flops=1600000000, bytes_accessed=24000000, transcendentals=0),
    )(tile_index[0], tile_count, tile_values[0], features)

    term = pl.pallas_call(
        weight_terms,
        out_shape=jax.ShapeDtypeStruct((n_rows, depth, width), jnp.bfloat16),
        in_specs=[VMEM, VMEM],
        out_specs=VMEM,
        compiler_params=params,
    )(mixed, received)
    terms = exchange(term, "rows")

    place = (lax.axis_index("rep") % RING).astype(jnp.int32)[None]
    full = jax.ShapeDtypeStruct((columns, size, width), jnp.float32)
    waiting = jax.ShapeDtypeStruct((3 * columns // 2, size // 2, width), jnp.float32)
    sent = jax.ShapeDtypeStruct((3 * columns // 2, size // 2, width), jnp.bfloat16)
    keep, up, down, ahead, behind = pl.pallas_call(
        products,
        out_shape=(full, sent, sent, waiting, waiting),
        in_specs=[SMEM, VMEM, HBM],
        out_specs=(VMEM,) * 5,
        scratch_shapes=[
            pltpu.VMEM((col_blocks * size, total_rows), jnp.bfloat16),
            pltpu.SemaphoreType.DMA((columns,)),
        ],
        compiler_params=params,
        cost_estimate=pl.CostEstimate(flops=1700000000, bytes_accessed=9000000, transcendentals=0),
    )(place, received, pltpu.with_memory_space_constraint(turned, pltpu.HBM))
    up, down = passed(up, 1), passed(down, -1)
    ahead, behind = pl.pallas_call(
        functools.partial(relay, columns),
        out_shape=(sent, sent),
        in_specs=[VMEM] * 4,
        out_specs=(VMEM, VMEM),
        compiler_params=params,
    )(ahead, behind, up, down)
    share = pl.pallas_call(
        spread_sum,
        out_shape=jax.ShapeDtypeStruct((n_rep, depth, width), jnp.bfloat16),
        in_specs=[VMEM, pl.BlockSpec(memory_space=pl.ANY)],
        out_specs=VMEM,
        compiler_params=params,
    )(terms, ahead)
    own = jnp.sum(exchange(share, "rep").astype(jnp.float32), axis=0)
    ahead, behind = passed(ahead, 1), passed(behind, -1)
    parts = pl.pallas_call(
        add_ring,
        out_shape=jax.ShapeDtypeStruct((columns, size, width), jnp.bfloat16),
        in_specs=[VMEM] * 5,
        out_specs=VMEM,
        compiler_params=params,
    )(keep, up, down, ahead, behind)
    parts = exchange(parts, "rep", axis_index_groups=groups)

    own = own.astype(jnp.bfloat16)
    pair = jnp.concatenate([own, swapped(own, 1, "rows")], axis=0)
    others = [swapped(pair, mask, "rows") for mask in (2, 4, 6)]
    return pl.pallas_call(
        finish,
        out_shape=(
            jax.ShapeDtypeStruct((node_dev, width), jnp.bfloat16),
            jax.ShapeDtypeStruct((width, width), jnp.float32),
        ),
        in_specs=[SMEM] + [VMEM] * 6,
        out_specs=(VMEM, VMEM),
        compiler_params=params,
    )((lax.axis_index("rows") % SLICES).astype(jnp.int32)[None], parts, weight, pair, *others)


def solution(mesh):
    return jax.shard_map(
        per_device,
        mesh=mesh,
        in_specs=(
            P(("rows", "rep"), None),
            P(("rows", "rep"), None),
            P("rows", None),
            P(),
            P(("rows", "rep"), None, None),
            P(("rows", "rep"), None),
            P(("rows", "rep"), None),
            P(("rows", "rep")),
            P(("rows", "rep"), None, None, None),
        ),
        out_specs=(P(("rows", "rep"), None), P()),
        check_vma=False,
    )
```

```python
import functools

import jax
import jax.numpy as jnp
from jax import lax
from jax.experimental import pallas as pl
from jax.experimental.pallas import tpu as pltpu
from jax.sharding import PartitionSpec as P

VMEM_BYTES = 24000000
PICK_VMEM_BYTES = 60000000
SLICES = 8
RING = 4
GROUPS = 2
SMEM = pl.BlockSpec(memory_space=pltpu.SMEM)
VMEM = pl.BlockSpec(memory_space=pltpu.VMEM)
HBM = pl.BlockSpec(memory_space=pltpu.HBM)


def pick_rows(count_ref, out_grad_ref, pre_relu_ref, send_rows_ref, out_ref):
    peers, slots = send_rows_ref.shape
    nodes = out_grad_ref.shape[0]
    grad_pre = jnp.where(pre_relu_ref[...] > 0, out_grad_ref[...], jnp.zeros_like(out_grad_ref))
    slot = lax.broadcasted_iota(jnp.int32, (1, slots), 1)
    node = lax.broadcasted_iota(jnp.int32, (nodes, nodes), 0)
    together = nodes // slots
    for first in range(0, peers, together):
        wanted = [
            jnp.where(slot < count_ref[q], send_rows_ref[q : q + 1, :], -1) for q in range(first, first + together)
        ]
        picks = jnp.where(node == jnp.concatenate(wanted, axis=1), 1.0, 0.0).astype(jnp.bfloat16)
        out_ref[first * slots : (first + together) * slots] = lax.dot_general(
            picks, grad_pre, (((0,), (0,)), ((), ())), preferred_element_type=jnp.float32
        ).astype(out_ref.dtype)


def place_tiles(index_ref, count_ref, tiles_ref, features_ref, turned_ref, mixed_ref, dense, turned, total, sem):
    col_blocks, row_blocks, size, _ = dense.shape
    dense[...] = jnp.zeros_like(dense)
    turned[...] = jnp.zeros_like(turned)
    total[...] = jnp.zeros_like(total)
    count = count_ref[0]

    def place(t, carry):
        k = index_ref[t]
        c, r = lax.rem(k, col_blocks), lax.div(k, col_blocks)
        tile = jnp.where(t < count, tiles_ref[t], jnp.zeros_like(tiles_ref[t]))
        dense[c, r] = tile
        first = pl.multiple_of(c * size, size)
        turned[pl.ds(first, size), pl.ds(pl.multiple_of(r * size, size), size)] = tile.T
        return carry

    lax.fori_loop(0, tiles_ref.shape[0], place, 0, unroll=4)
    copy = pltpu.make_async_copy(turned, turned_ref, sem)
    copy.start()

    def mix(j, carry):
        left = dense[2 * j].reshape(row_blocks * size, size)
        right = dense[2 * j + 1].reshape(row_blocks * size, size)
        total[...] += jnp.dot(
            jnp.concatenate([left, right], axis=1),
            features_ref[pl.ds(pl.multiple_of(2 * j * size, 2 * size), 2 * size), :],
            preferred_element_type=jnp.float32,
        )
        return carry

    lax.fori_loop(0, col_blocks // 2, mix, 0)
    mixed_ref[...] = total[...].astype(mixed_ref.dtype).T
    copy.wait()


def weight_terms(mixed_ref, rows_ref, out_ref):
    depth, width = out_ref.shape[1:]
    slices = mixed_ref.shape[0] // depth
    term = jnp.dot(mixed_ref[...], rows_ref[...], preferred_element_type=jnp.float32)
    term = term.astype(out_ref.dtype).reshape(slices, depth, width)
    for first in range(0, out_ref.shape[0], slices):
        out_ref[first : first + slices] = term


def share_sum(place_ref, own_ref, behind_ref, ahead_ref, far_ref, out_ref, shares):
    place = place_ref[0]
    for distance, ref in enumerate((own_ref, ahead_ref, far_ref, behind_ref)):
        shares[(place + distance) & (RING - 1)] = ref[...].astype(jnp.float32)
    total = ((shares[0] + shares[1]) + (shares[2] + shares[3])).astype(out_ref.dtype)
    for y in range(out_ref.shape[0]):
        out_ref[y] = total


def products(
    place_ref, rows_ref, turned_ref, keep_ref, up_ref, down_ref, up_rest_ref, down_rest_ref, next_ref, last_ref, turned, sems
):
    groups, size, _ = keep_ref.shape
    half = size // 2
    place = place_ref[0]
    copies = []
    for g in range(groups):
        span = pl.ds(RING * g * size, RING * size)
        copies.append(pltpu.make_async_copy(turned_ref.at[span], turned.at[span], sems.at[g]))
        copies[-1].start()
    for first in range(0, groups, GROUPS):
        taken = []
        for g in range(first, first + GROUPS):
            copies[g].wait()
            for ahead in range(RING):
                c = RING * g + ((place + ahead) & (RING - 1))
                taken.append(turned[pl.ds(pl.multiple_of(c * size, size), size), :])
        part = jnp.dot(jnp.concatenate(taken, axis=0), rows_ref[...], preferred_element_type=jnp.float32)
        for i in range(GROUPS):
            own, one, two, three = [part[(RING * i + j) * size : (RING * i + j + 1) * size] for j in range(RING)]
            g = first + i
            keep_ref[g] = own
            up_ref[g] = two[:half].astype(up_ref.dtype)
            down_ref[g] = two[half:].astype(down_ref.dtype)
            next_ref[g] = one[:half]
            last_ref[g] = three[half:]
            if g < groups // 2:
                up_ref[groups + g] = one[half:].astype(up_ref.dtype)
                down_ref[groups + g] = three[:half].astype(down_ref.dtype)
            else:
                up_rest_ref[g - groups // 2] = one[half:].astype(up_ref.dtype)
                down_rest_ref[g - groups // 2] = three[:half].astype(down_ref.dtype)


def relay(terms_ref, next_ref, last_ref, up_ref, down_ref, next_out_ref, last_out_ref, share_ref):
    groups, half, _ = next_ref.shape
    for g in range(groups):
        rows = slice(g * half, (g + 1) * half)
        next_out_ref[rows] = (next_ref[g] + up_ref[g].astype(jnp.float32)).astype(next_out_ref.dtype)
        last_out_ref[rows] = (last_ref[g] + down_ref[g].astype(jnp.float32)).astype(last_out_ref.dtype)
    total = terms_ref[0].astype(jnp.float32)
    for i in range(1, terms_ref.shape[0]):
        total += terms_ref[i].astype(jnp.float32)
    total = total.astype(share_ref.dtype)
    share_ref[...] = total
    next_out_ref[groups * half :] = total
    last_out_ref[groups * half :] = total


def add_ring(keep_ref, up_ref, down_ref, up_rest_ref, down_rest_ref, next_ref, last_ref, out_ref):
    groups, size, _ = keep_ref.shape
    half = size // 2
    for g in range(groups):
        if g < groups // 2:
            from_last, from_next = up_ref[groups + g], down_ref[groups + g]
        else:
            from_last, from_next = up_rest_ref[g - groups // 2], down_rest_ref[g - groups // 2]
        rows = slice(g * half, (g + 1) * half)
        low = keep_ref[g, :half] + from_next.astype(jnp.float32) + next_ref[rows].astype(jnp.float32)
        high = keep_ref[g, half:] + from_last.astype(jnp.float32) + last_ref[rows].astype(jnp.float32)
        out_ref[g, :half] = low.astype(out_ref.dtype)
        out_ref[g, half:] = high.astype(out_ref.dtype)


def finish(place_ref, parts_ref, weight_ref, pair_ref, two_ref, four_ref, six_ref, feature_grad_ref, weight_grad_ref):
    grads = parts_ref[0].astype(jnp.float32)
    for y in range(1, parts_ref.shape[0]):
        grads += parts_ref[y].astype(jnp.float32)
    feature_grad_ref[...] = lax.dot_general(
        grads.astype(jnp.bfloat16), weight_ref[...], (((1,), (1,)), ((), ())), preferred_element_type=jnp.float32
    ).astype(feature_grad_ref.dtype)
    depth = pair_ref.shape[0] // 2
    for j in range(SLICES):
        piece_ref = (pair_ref, two_ref, four_ref, six_ref)[j // 2]
        first = pl.multiple_of((place_ref[0] ^ j) * depth, depth)
        piece = piece_ref[(j % 2) * depth : (j % 2 + 1) * depth]
        weight_grad_ref[pl.ds(first, depth), :] = piece.astype(weight_grad_ref.dtype)


def per_device(
    out_grad, pre_relu, features, weight, send_rows, send_count, tile_index, tile_count, tile_values
):
    node_dev, width = out_grad.shape
    n_rows = lax.axis_size("rows")
    n_rep = lax.axis_size("rep")
    per_peer = send_rows.shape[2]
    size = tile_values.shape[2]
    col_blocks = features.shape[0] // size
    total_rows = n_rows * per_peer
    row_blocks = total_rows // size
    depth = width // SLICES
    columns = col_blocks // RING
    groups = [list(range(x, n_rep, RING)) for x in range(RING)]
    exchange = functools.partial(lax.all_to_all, split_axis=0, concat_axis=0, tiled=True)
    params = pltpu.CompilerParams(vmem_limit_bytes=VMEM_BYTES)

    def swapped(value, mask, axis="rep"):
        return lax.ppermute(value, axis, [(i, i ^ mask) for i in range(lax.axis_size(axis))])

    def passed(value, step):
        return lax.ppermute(value, "rep", [(i, i - i % RING + (i + step) % RING) for i in range(n_rep)])

    outgoing = pl.pallas_call(
        pick_rows,
        out_shape=jax.ShapeDtypeStruct((total_rows, width), jnp.bfloat16),
        in_specs=[SMEM, VMEM, VMEM, VMEM],
        out_specs=VMEM,
        compiler_params=pltpu.CompilerParams(vmem_limit_bytes=PICK_VMEM_BYTES),
    )(send_count[0], out_grad, pre_relu, send_rows[0])
    received = exchange(outgoing.reshape(n_rows, per_peer, width), "rows").reshape(total_rows, width)

    turned, mixed = pl.pallas_call(
        place_tiles,
        out_shape=(
            pltpu.HBM((col_blocks * size, total_rows), jnp.bfloat16),
            jax.ShapeDtypeStruct((width, total_rows), jnp.bfloat16),
        ),
        in_specs=[SMEM, SMEM, VMEM, VMEM],
        out_specs=(HBM, VMEM),
        scratch_shapes=[
            pltpu.VMEM((col_blocks, row_blocks, size, size), jnp.bfloat16),
            pltpu.VMEM((col_blocks * size, total_rows), jnp.bfloat16),
            pltpu.VMEM((total_rows, width), jnp.float32),
            pltpu.SemaphoreType.DMA,
        ],
        compiler_params=params,
        cost_estimate=pl.CostEstimate(flops=1600000000, bytes_accessed=24000000, transcendentals=0),
    )(tile_index[0], tile_count, tile_values[0], features)

    term = pl.pallas_call(
        weight_terms,
        out_shape=jax.ShapeDtypeStruct((n_rows, depth, width), jnp.bfloat16),
        in_specs=[VMEM, VMEM],
        out_specs=VMEM,
        compiler_params=params,
    )(mixed, received)
    terms = exchange(term, "rows")

    place = (lax.axis_index("rep") % RING).astype(jnp.int32)[None]
    full = jax.ShapeDtypeStruct((columns, size, width), jnp.float32)
    waiting = jax.ShapeDtypeStruct((columns, size // 2, width), jnp.float32)
    sent = jax.ShapeDtypeStruct((3 * columns // 2, size // 2, width), jnp.bfloat16)
    rest = jax.ShapeDtypeStruct((columns // 2, size // 2, width), jnp.bfloat16)
    passed_on = jax.ShapeDtypeStruct((columns * size // 2 + depth, width), jnp.bfloat16)
    share = jax.ShapeDtypeStruct((depth, width), jnp.bfloat16)
    keep, up, down, up_rest, down_rest, ahead, behind = pl.pallas_call(
        products,
        out_shape=(full, sent, sent, rest, rest, waiting, waiting),
        in_specs=[SMEM, VMEM, HBM],
        out_specs=(VMEM,) * 7,
        scratch_shapes=[
            pltpu.VMEM((col_blocks * size, total_rows), jnp.bfloat16),
            pltpu.SemaphoreType.DMA((columns,)),
        ],
        compiler_params=params,
        cost_estimate=pl.CostEstimate(flops=1700000000, bytes_accessed=9000000, transcendentals=0),
    )(place, received, pltpu.with_memory_space_constraint(turned, pltpu.HBM))
    up, down = passed(up, 1), passed(down, -1)
    ahead, behind, own = pl.pallas_call(
        relay,
        out_shape=(passed_on, passed_on, share),
        in_specs=[VMEM] * 5,
        out_specs=(VMEM,) * 3,
        compiler_params=params,
    )(terms, ahead, behind, up, down)
    ahead, behind, far = passed(ahead, 1), passed(behind, -1), passed(own, 2)
    share_spec = pl.BlockSpec((depth, width), lambda i: (0, 0))
    tail_spec = pl.BlockSpec((depth, width), lambda i: (columns * size // 2 // depth, 0))
    shares = pl.pallas_call(
        share_sum,
        grid=(1,),
        out_shape=jax.ShapeDtypeStruct((columns, depth, width), jnp.bfloat16),
        in_specs=[SMEM, share_spec, tail_spec, tail_spec, share_spec],
        out_specs=pl.BlockSpec((columns, depth, width), lambda i: (0, 0, 0)),
        scratch_shapes=[pltpu.VMEM((RING, depth, width), jnp.float32)],
        compiler_params=params,
    )(place, own, ahead, behind, far)
    own = jnp.sum(exchange(shares, "rep", axis_index_groups=groups).astype(jnp.float32), axis=0)
    up_rest, down_rest = passed(up_rest, 1), passed(down_rest, -1)
    parts = pl.pallas_call(
        add_ring,
        out_shape=jax.ShapeDtypeStruct((columns, size, width), jnp.bfloat16),
        in_specs=[VMEM] * 7,
        out_specs=VMEM,
        compiler_params=params,
    )(keep, up, down, up_rest, down_rest, ahead, behind)
    parts = exchange(parts, "rep", axis_index_groups=groups)

    own = own.astype(jnp.bfloat16)
    pair = jnp.concatenate([own, swapped(own, 1, "rows")], axis=0)
    others = [swapped(pair, mask, "rows") for mask in (2, 4, 6)]
    return pl.pallas_call(
        finish,
        out_shape=(
            jax.ShapeDtypeStruct((node_dev, width), jnp.bfloat16),
            jax.ShapeDtypeStruct((width, width), jnp.float32),
        ),
        in_specs=[SMEM] + [VMEM] * 6,
        out_specs=(VMEM, VMEM),
        compiler_params=params,
    )((lax.axis_index("rows") % SLICES).astype(jnp.int32)[None], parts, weight, pair, *others)


def solution(mesh):
    return jax.shard_map(
        per_device,
        mesh=mesh,
        in_specs=(
            P(("rows", "rep"), None),
            P(("rows", "rep"), None),
            P("rows", None),
            P(),
            P(("rows", "rep"), None, None),
            P(("rows", "rep"), None),
            P(("rows", "rep"), None),
            P(("rows", "rep")),
            P(("rows", "rep"), None, None, None),
        ),
        out_specs=(P(("rows", "rep"), None), P()),
        check_vma=False,
    )
```

```python
import functools

import jax
import jax.numpy as jnp
from jax import lax
from jax.experimental import pallas as pl
from jax.experimental.pallas import tpu as pltpu
from jax.sharding import PartitionSpec as P

VMEM_BYTES = 24000000
PICK_VMEM_BYTES = 60000000
SLICES = 8
RING = 4
GROUPS = 2
SMEM = pl.BlockSpec(memory_space=pltpu.SMEM)
VMEM = pl.BlockSpec(memory_space=pltpu.VMEM)
HBM = pl.BlockSpec(memory_space=pltpu.HBM)


def pick_rows(count_ref, out_grad_ref, pre_relu_ref, send_rows_ref, out_ref):
    peers, slots = send_rows_ref.shape
    nodes = out_grad_ref.shape[0]
    grad_pre = jnp.where(pre_relu_ref[...] > 0, out_grad_ref[...], jnp.zeros_like(out_grad_ref))
    slot = lax.broadcasted_iota(jnp.int32, (1, slots), 1)
    node = lax.broadcasted_iota(jnp.int32, (nodes, nodes), 0)
    together = nodes // slots
    for first in range(0, peers, together):
        wanted = [
            jnp.where(slot < count_ref[q], send_rows_ref[q : q + 1, :], -1) for q in range(first, first + together)
        ]
        picks = jnp.where(node == jnp.concatenate(wanted, axis=1), 1.0, 0.0).astype(jnp.bfloat16)
        out_ref[first * slots : (first + together) * slots] = lax.dot_general(
            picks, grad_pre, (((0,), (0,)), ((), ())), preferred_element_type=jnp.float32
        ).astype(out_ref.dtype)


def place_tiles(index_ref, count_ref, tiles_ref, features_ref, turned_ref, mixed_ref, dense, turned, total, sem):
    col_blocks, row_blocks, size, _ = dense.shape
    dense[...] = jnp.zeros_like(dense)
    turned[...] = jnp.zeros_like(turned)
    total[...] = jnp.zeros_like(total)
    count = count_ref[0]

    def place(t, carry):
        k = index_ref[t]
        c, r = lax.rem(k, col_blocks), lax.div(k, col_blocks)
        tile = jnp.where(t < count, tiles_ref[t], jnp.zeros_like(tiles_ref[t]))
        dense[c, r] = tile
        first = pl.multiple_of(c * size, size)
        turned[pl.ds(first, size), pl.ds(pl.multiple_of(r * size, size), size)] = tile.T
        return carry

    lax.fori_loop(0, tiles_ref.shape[0], place, 0, unroll=4)
    copy = pltpu.make_async_copy(turned, turned_ref, sem)
    copy.start()

    def mix(j, carry):
        left = dense[2 * j].reshape(row_blocks * size, size)
        right = dense[2 * j + 1].reshape(row_blocks * size, size)
        total[...] += jnp.dot(
            jnp.concatenate([left, right], axis=1),
            features_ref[pl.ds(pl.multiple_of(2 * j * size, 2 * size), 2 * size), :],
            preferred_element_type=jnp.float32,
        )
        return carry

    lax.fori_loop(0, col_blocks // 2, mix, 0)
    mixed_ref[...] = total[...].astype(mixed_ref.dtype).T
    copy.wait()


def weight_terms(mixed_ref, rows_ref, out_ref):
    depth, width = out_ref.shape[1:]
    slices = mixed_ref.shape[0] // depth
    term = jnp.dot(mixed_ref[...], rows_ref[...], preferred_element_type=jnp.float32)
    term = term.astype(out_ref.dtype).reshape(slices, depth, width)
    for first in range(0, out_ref.shape[0], slices):
        out_ref[first : first + slices] = term


def ring_sum(place_ref, own_ref, ahead_ref, far_ref, behind_ref, out_ref, shares):
    place = place_ref[0]
    for distance, ref in enumerate((own_ref, ahead_ref, far_ref, behind_ref)):
        shares[(place + distance) & (RING - 1)] = ref[...]
    out_ref[...] = ((shares[0] + shares[1]) + (shares[2] + shares[3])).astype(out_ref.dtype)


def products(place_ref, rows_ref, turned_ref, keep_ref, up_ref, down_ref, next_ref, last_ref, turned, sems):
    groups, size, _ = keep_ref.shape
    half = size // 2
    place = place_ref[0]
    copies = []
    for g in range(groups):
        span = pl.ds(RING * g * size, RING * size)
        copies.append(pltpu.make_async_copy(turned_ref.at[span], turned.at[span], sems.at[g]))
        copies[-1].start()
    for first in range(0, groups, GROUPS):
        taken = []
        for g in range(first, first + GROUPS):
            copies[g].wait()
            for ahead in range(RING):
                c = RING * g + ((place + ahead) & (RING - 1))
                taken.append(turned[pl.ds(pl.multiple_of(c * size, size), size), :])
        part = jnp.dot(jnp.concatenate(taken, axis=0), rows_ref[...], preferred_element_type=jnp.float32)
        for i in range(GROUPS):
            own, one, two, three = [part[(RING * i + j) * size : (RING * i + j + 1) * size] for j in range(RING)]
            g = first + i
            keep_ref[g] = own
            up_ref[g] = two[:half].astype(up_ref.dtype)
            down_ref[g] = two[half:].astype(down_ref.dtype)
            next_ref[g] = one[:half]
            last_ref[g] = three[half:]
            if g < groups // 2:
                up_ref[groups + g] = one[half:].astype(up_ref.dtype)
                down_ref[groups + g] = three[:half].astype(down_ref.dtype)
            else:
                next_ref[groups // 2 + g] = one[half:]
                last_ref[groups // 2 + g] = three[:half]


def relay(terms_ref, next_ref, last_ref, up_ref, down_ref, next_out_ref, last_out_ref, share_ref):
    groups = share_ref.shape[0]
    for g in range(groups):
        next_out_ref[g] = (next_ref[g] + up_ref[g].astype(jnp.float32)).astype(next_out_ref.dtype)
        last_out_ref[g] = (last_ref[g] + down_ref[g].astype(jnp.float32)).astype(last_out_ref.dtype)
    for g in range(groups, next_ref.shape[0]):
        next_out_ref[g] = next_ref[g].astype(next_out_ref.dtype)
        last_out_ref[g] = last_ref[g].astype(last_out_ref.dtype)
    total = terms_ref[0].astype(jnp.float32)
    for i in range(1, terms_ref.shape[0]):
        total += terms_ref[i].astype(jnp.float32)
    for y in range(groups):
        share_ref[y] = total.astype(share_ref.dtype)


def add_ring(keep_ref, up_ref, down_ref, next_ref, last_ref, after_ref, out_ref):
    del after_ref
    groups, size, _ = keep_ref.shape
    half = size // 2
    for g in range(groups):
        if g < groups // 2:
            from_last, from_next = up_ref[groups + g], down_ref[groups + g]
        else:
            from_last, from_next = next_ref[groups // 2 + g], last_ref[groups // 2 + g]
        low = keep_ref[g, :half] + from_next.astype(jnp.float32) + next_ref[g].astype(jnp.float32)
        high = keep_ref[g, half:] + from_last.astype(jnp.float32) + last_ref[g].astype(jnp.float32)
        out_ref[g, :half] = low.astype(out_ref.dtype)
        out_ref[g, half:] = high.astype(out_ref.dtype)


def finish(place_ref, parts_ref, weight_ref, pair_ref, two_ref, four_ref, six_ref, feature_grad_ref, weight_grad_ref):
    grads = parts_ref[0].astype(jnp.float32)
    for y in range(1, parts_ref.shape[0]):
        grads += parts_ref[y].astype(jnp.float32)
    feature_grad_ref[...] = lax.dot_general(
        grads.astype(jnp.bfloat16), weight_ref[...], (((1,), (1,)), ((), ())), preferred_element_type=jnp.float32
    ).astype(feature_grad_ref.dtype)
    depth = pair_ref.shape[0] // 2
    for j in range(SLICES):
        piece_ref = (pair_ref, two_ref, four_ref, six_ref)[j // 2]
        first = pl.multiple_of((place_ref[0] ^ j) * depth, depth)
        piece = piece_ref[(j % 2) * depth : (j % 2 + 1) * depth]
        weight_grad_ref[pl.ds(first, depth), :] = piece.astype(weight_grad_ref.dtype)


def per_device(
    out_grad, pre_relu, features, weight, send_rows, send_count, tile_index, tile_count, tile_values
):
    node_dev, width = out_grad.shape
    n_rows = lax.axis_size("rows")
    n_rep = lax.axis_size("rep")
    per_peer = send_rows.shape[2]
    size = tile_values.shape[2]
    col_blocks = features.shape[0] // size
    total_rows = n_rows * per_peer
    row_blocks = total_rows // size
    depth = width // SLICES
    columns = col_blocks // RING
    groups = [list(range(x, n_rep, RING)) for x in range(RING)]
    exchange = functools.partial(lax.all_to_all, split_axis=0, concat_axis=0, tiled=True)
    params = pltpu.CompilerParams(vmem_limit_bytes=VMEM_BYTES)

    def swapped(value, mask, axis="rep"):
        return lax.ppermute(value, axis, [(i, i ^ mask) for i in range(lax.axis_size(axis))])

    def passed(value, step):
        return lax.ppermute(value, "rep", [(i, i - i % RING + (i + step) % RING) for i in range(n_rep)])

    outgoing = pl.pallas_call(
        pick_rows,
        out_shape=jax.ShapeDtypeStruct((total_rows, width), jnp.bfloat16),
        in_specs=[SMEM, VMEM, VMEM, VMEM],
        out_specs=VMEM,
        compiler_params=pltpu.CompilerParams(vmem_limit_bytes=PICK_VMEM_BYTES),
    )(send_count[0], out_grad, pre_relu, send_rows[0])
    received = exchange(outgoing.reshape(n_rows, per_peer, width), "rows").reshape(total_rows, width)

    turned, mixed = pl.pallas_call(
        place_tiles,
        out_shape=(
            pltpu.HBM((col_blocks * size, total_rows), jnp.bfloat16),
            jax.ShapeDtypeStruct((width, total_rows), jnp.bfloat16),
        ),
        in_specs=[SMEM, SMEM, VMEM, VMEM],
        out_specs=(HBM, VMEM),
        scratch_shapes=[
            pltpu.VMEM((col_blocks, row_blocks, size, size), jnp.bfloat16),
            pltpu.VMEM((col_blocks * size, total_rows), jnp.bfloat16),
            pltpu.VMEM((total_rows, width), jnp.float32),
            pltpu.SemaphoreType.DMA,
        ],
        compiler_params=params,
        cost_estimate=pl.CostEstimate(flops=1600000000, bytes_accessed=24000000, transcendentals=0),
    )(tile_index[0], tile_count, tile_values[0], features)

    term = pl.pallas_call(
        weight_terms,
        out_shape=jax.ShapeDtypeStruct((n_rows, depth, width), jnp.bfloat16),
        in_specs=[VMEM, VMEM],
        out_specs=VMEM,
        compiler_params=params,
    )(mixed, received)
    terms = exchange(term, "rows")

    place = (lax.axis_index("rep") % RING).astype(jnp.int32)[None]
    full = jax.ShapeDtypeStruct((columns, size, width), jnp.float32)
    waiting = jax.ShapeDtypeStruct((3 * columns // 2, size // 2, width), jnp.float32)
    sent = jax.ShapeDtypeStruct((3 * columns // 2, size // 2, width), jnp.bfloat16)
    keep, up, down, ahead, behind = pl.pallas_call(
        products,
        out_shape=(full, sent, sent, waiting, waiting),
        in_specs=[SMEM, VMEM, HBM],
        out_specs=(VMEM,) * 5,
        scratch_shapes=[
            pltpu.VMEM((col_blocks * size, total_rows), jnp.bfloat16),
            pltpu.SemaphoreType.DMA((columns,)),
        ],
        compiler_params=params,
        cost_estimate=pl.CostEstimate(flops=1700000000, bytes_accessed=9000000, transcendentals=0),
    )(place, received, pltpu.with_memory_space_constraint(turned, pltpu.HBM))
    up, down = passed(up, 1), passed(down, -1)
    ahead, behind, shares = pl.pallas_call(
        relay,
        out_shape=(sent, sent, jax.ShapeDtypeStruct((columns, depth, width), jnp.bfloat16)),
        in_specs=[VMEM] * 5,
        out_specs=(VMEM,) * 3,
        compiler_params=params,
    )(terms, ahead, behind, up, down)
    own = jnp.sum(exchange(shares, "rep", axis_index_groups=groups).astype(jnp.float32), axis=0)
    ahead, behind = passed(ahead, 1), passed(behind, -1)
    own = pl.pallas_call(
        ring_sum,
        out_shape=jax.ShapeDtypeStruct((depth, width), jnp.bfloat16),
        in_specs=[SMEM] + [VMEM] * 4,
        out_specs=VMEM,
        scratch_shapes=[pltpu.VMEM((RING, depth, width), jnp.float32)],
        compiler_params=params,
    )(place, own, passed(own, -1), passed(own, 2), passed(own, 1))
    parts = pl.pallas_call(
        add_ring,
        out_shape=jax.ShapeDtypeStruct((columns, size, width), jnp.bfloat16),
        in_specs=[VMEM] * 5 + [pl.BlockSpec(memory_space=pl.ANY)],
        out_specs=VMEM,
        compiler_params=params,
    )(keep, up, down, ahead, behind, own)
    parts = exchange(parts, "rep", axis_index_groups=groups)

    pair = jnp.concatenate([own, swapped(own, 1, "rows")], axis=0)
    others = [swapped(pair, mask, "rows") for mask in (2, 4, 6)]
    return pl.pallas_call(
        finish,
        out_shape=(
            jax.ShapeDtypeStruct((node_dev, width), jnp.bfloat16),
            jax.ShapeDtypeStruct((width, width), jnp.float32),
        ),
        in_specs=[SMEM] + [VMEM] * 6,
        out_specs=(VMEM, VMEM),
        compiler_params=params,
    )((lax.axis_index("rows") % SLICES).astype(jnp.int32)[None], parts, weight, pair, *others)


def solution(mesh):
    return jax.shard_map(
        per_device,
        mesh=mesh,
        in_specs=(
            P(("rows", "rep"), None),
            P(("rows", "rep"), None),
            P("rows", None),
            P(),
            P(("rows", "rep"), None, None),
            P(("rows", "rep"), None),
            P(("rows", "rep"), None),
            P(("rows", "rep")),
            P(("rows", "rep"), None, None, None),
        ),
        out_specs=(P(("rows", "rep"), None), P()),
        check_vma=False,
    )
```

```python
import functools

import jax
import jax.numpy as jnp
from jax import lax
from jax.experimental import pallas as pl
from jax.experimental.pallas import tpu as pltpu
from jax.sharding import PartitionSpec as P

VMEM_BYTES = 24000000
PICK_VMEM_BYTES = 60000000
SLICES = 8
RING = 4
GROUPS = 2
SMEM = pl.BlockSpec(memory_space=pltpu.SMEM)
VMEM = pl.BlockSpec(memory_space=pltpu.VMEM)
HBM = pl.BlockSpec(memory_space=pltpu.HBM)


def pick_rows(count_ref, out_grad_ref, pre_relu_ref, send_rows_ref, out_ref):
    peers, slots = send_rows_ref.shape
    nodes = out_grad_ref.shape[0]
    grad_pre = jnp.where(pre_relu_ref[...] > 0, out_grad_ref[...], jnp.zeros_like(out_grad_ref))
    slot = lax.broadcasted_iota(jnp.int32, (1, slots), 1)
    node = lax.broadcasted_iota(jnp.int32, (nodes, nodes), 0)
    together = nodes // slots
    for first in range(0, peers, together):
        wanted = [
            jnp.where(slot < count_ref[q], send_rows_ref[q : q + 1, :], -1) for q in range(first, first + together)
        ]
        picks = jnp.where(node == jnp.concatenate(wanted, axis=1), 1.0, 0.0).astype(jnp.bfloat16)
        out_ref[first * slots : (first + together) * slots] = lax.dot_general(
            picks, grad_pre, (((0,), (0,)), ((), ())), preferred_element_type=jnp.float32
        ).astype(out_ref.dtype)


def place_tiles(index_ref, count_ref, tiles_ref, features_ref, turned_ref, mixed_ref, dense, turned, total, sem):
    col_blocks, row_blocks, size, _ = dense.shape
    dense[...] = jnp.zeros_like(dense)
    turned[...] = jnp.zeros_like(turned)
    total[...] = jnp.zeros_like(total)
    count = count_ref[0]

    def place(t, carry):
        k = index_ref[t]
        c, r = lax.rem(k, col_blocks), lax.div(k, col_blocks)
        tile = jnp.where(t < count, tiles_ref[t], jnp.zeros_like(tiles_ref[t]))
        dense[c, r] = tile
        first = pl.multiple_of(c * size, size)
        turned[pl.ds(first, size), pl.ds(pl.multiple_of(r * size, size), size)] = tile.T
        return carry

    lax.fori_loop(0, tiles_ref.shape[0], place, 0, unroll=4)
    copy = pltpu.make_async_copy(turned, turned_ref, sem)
    copy.start()

    def mix(j, carry):
        left = dense[2 * j].reshape(row_blocks * size, size)
        right = dense[2 * j + 1].reshape(row_blocks * size, size)
        total[...] += jnp.dot(
            jnp.concatenate([left, right], axis=1),
            features_ref[pl.ds(pl.multiple_of(2 * j * size, 2 * size), 2 * size), :],
            preferred_element_type=jnp.float32,
        )
        return carry

    lax.fori_loop(0, col_blocks // 2, mix, 0)
    mixed_ref[...] = total[...].astype(mixed_ref.dtype).T
    copy.wait()


def weight_terms(mixed_ref, rows_ref, out_ref):
    depth, width = out_ref.shape[1:]
    slices = mixed_ref.shape[0] // depth
    term = jnp.dot(mixed_ref[...], rows_ref[...], preferred_element_type=jnp.float32)
    term = term.astype(out_ref.dtype).reshape(slices, depth, width)
    for first in range(0, out_ref.shape[0], slices):
        out_ref[first : first + slices] = term


def share_sum(place_ref, own_ref, behind_ref, ahead_ref, far_ref, out_ref, shares):
    place = place_ref[0]
    for distance, ref in enumerate((own_ref, ahead_ref, far_ref, behind_ref)):
        shares[(place + distance) & (RING - 1)] = ref[...].astype(jnp.float32)
    total = ((shares[0] + shares[1]) + (shares[2] + shares[3])).astype(out_ref.dtype)
    for y in range(out_ref.shape[0]):
        out_ref[y] = total


def products(place_ref, rows_ref, turned_ref, keep_ref, up_ref, down_ref, next_ref, last_ref, turned, sems):
    groups, size, _ = keep_ref.shape
    half = size // 2
    place = place_ref[0]
    copies = []
    for g in range(groups):
        span = pl.ds(RING * g * size, RING * size)
        copies.append(pltpu.make_async_copy(turned_ref.at[span], turned.at[span], sems.at[g]))
        copies[-1].start()
    for first in range(0, groups, GROUPS):
        taken = []
        for g in range(first, first + GROUPS):
            copies[g].wait()
            for ahead in range(RING):
                c = RING * g + ((place + ahead) & (RING - 1))
                taken.append(turned[pl.ds(pl.multiple_of(c * size, size), size), :])
        part = jnp.dot(jnp.concatenate(taken, axis=0), rows_ref[...], preferred_element_type=jnp.float32)
        for i in range(GROUPS):
            own, one, two, three = [part[(RING * i + j) * size : (RING * i + j + 1) * size] for j in range(RING)]
            g = first + i
            keep_ref[g] = own
            up_ref[g] = two[:half].astype(up_ref.dtype)
            down_ref[g] = two[half:].astype(down_ref.dtype)
            next_ref[g] = one[:half]
            last_ref[g] = three[half:]
            up_ref[groups + g] = one[half:].astype(up_ref.dtype)
            down_ref[groups + g] = three[:half].astype(down_ref.dtype)


def relay(terms_ref, next_ref, last_ref, up_ref, down_ref, next_out_ref, last_out_ref, share_ref):
    groups, half, _ = next_ref.shape
    for g in range(groups):
        rows = slice(g * half, (g + 1) * half)
        next_out_ref[rows] = (next_ref[g] + up_ref[g].astype(jnp.float32)).astype(next_out_ref.dtype)
        last_out_ref[rows] = (last_ref[g] + down_ref[g].astype(jnp.float32)).astype(last_out_ref.dtype)
    total = terms_ref[0].astype(jnp.float32)
    for i in range(1, terms_ref.shape[0]):
        total += terms_ref[i].astype(jnp.float32)
    total = total.astype(share_ref.dtype)
    share_ref[...] = total
    next_out_ref[groups * half :] = total
    last_out_ref[groups * half :] = total


def add_ring(keep_ref, up_ref, down_ref, next_ref, last_ref, out_ref):
    groups, size, _ = keep_ref.shape
    half = size // 2
    for g in range(groups):
        rows = slice(g * half, (g + 1) * half)
        low = keep_ref[g, :half] + down_ref[groups + g].astype(jnp.float32) + next_ref[rows].astype(jnp.float32)
        high = keep_ref[g, half:] + up_ref[groups + g].astype(jnp.float32) + last_ref[rows].astype(jnp.float32)
        out_ref[g, :half] = low.astype(out_ref.dtype)
        out_ref[g, half:] = high.astype(out_ref.dtype)


def finish(place_ref, parts_ref, weight_ref, pair_ref, two_ref, four_ref, six_ref, feature_grad_ref, weight_grad_ref):
    grads = parts_ref[0].astype(jnp.float32)
    for y in range(1, parts_ref.shape[0]):
        grads += parts_ref[y].astype(jnp.float32)
    feature_grad_ref[...] = lax.dot_general(
        grads.astype(jnp.bfloat16), weight_ref[...], (((1,), (1,)), ((), ())), preferred_element_type=jnp.float32
    ).astype(feature_grad_ref.dtype)
    depth = pair_ref.shape[0] // 2
    for j in range(SLICES):
        piece_ref = (pair_ref, two_ref, four_ref, six_ref)[j // 2]
        first = pl.multiple_of((place_ref[0] ^ j) * depth, depth)
        piece = piece_ref[(j % 2) * depth : (j % 2 + 1) * depth]
        weight_grad_ref[pl.ds(first, depth), :] = piece.astype(weight_grad_ref.dtype)


def per_device(
    out_grad, pre_relu, features, weight, send_rows, send_count, tile_index, tile_count, tile_values
):
    node_dev, width = out_grad.shape
    n_rows = lax.axis_size("rows")
    n_rep = lax.axis_size("rep")
    per_peer = send_rows.shape[2]
    size = tile_values.shape[2]
    col_blocks = features.shape[0] // size
    total_rows = n_rows * per_peer
    row_blocks = total_rows // size
    depth = width // SLICES
    columns = col_blocks // RING
    groups = [list(range(x, n_rep, RING)) for x in range(RING)]
    exchange = functools.partial(lax.all_to_all, split_axis=0, concat_axis=0, tiled=True)
    params = pltpu.CompilerParams(vmem_limit_bytes=VMEM_BYTES)

    def swapped(value, mask, axis="rep"):
        return lax.ppermute(value, axis, [(i, i ^ mask) for i in range(lax.axis_size(axis))])

    def passed(value, step):
        return lax.ppermute(value, "rep", [(i, i - i % RING + (i + step) % RING) for i in range(n_rep)])

    outgoing = pl.pallas_call(
        pick_rows,
        out_shape=jax.ShapeDtypeStruct((total_rows, width), jnp.bfloat16),
        in_specs=[SMEM, VMEM, VMEM, VMEM],
        out_specs=VMEM,
        compiler_params=pltpu.CompilerParams(vmem_limit_bytes=PICK_VMEM_BYTES),
    )(send_count[0], out_grad, pre_relu, send_rows[0])
    received = exchange(outgoing.reshape(n_rows, per_peer, width), "rows").reshape(total_rows, width)

    turned, mixed = pl.pallas_call(
        place_tiles,
        out_shape=(
            pltpu.HBM((col_blocks * size, total_rows), jnp.bfloat16),
            jax.ShapeDtypeStruct((width, total_rows), jnp.bfloat16),
        ),
        in_specs=[SMEM, SMEM, VMEM, VMEM],
        out_specs=(HBM, VMEM),
        scratch_shapes=[
            pltpu.VMEM((col_blocks, row_blocks, size, size), jnp.bfloat16),
            pltpu.VMEM((col_blocks * size, total_rows), jnp.bfloat16),
            pltpu.VMEM((total_rows, width), jnp.float32),
            pltpu.SemaphoreType.DMA,
        ],
        compiler_params=params,
        cost_estimate=pl.CostEstimate(flops=1600000000, bytes_accessed=24000000, transcendentals=0),
    )(tile_index[0], tile_count, tile_values[0], features)

    term = pl.pallas_call(
        weight_terms,
        out_shape=jax.ShapeDtypeStruct((n_rows, depth, width), jnp.bfloat16),
        in_specs=[VMEM, VMEM],
        out_specs=VMEM,
        compiler_params=params,
    )(mixed, received)
    terms = exchange(term, "rows")

    place = (lax.axis_index("rep") % RING).astype(jnp.int32)[None]
    full = jax.ShapeDtypeStruct((columns, size, width), jnp.float32)
    waiting = jax.ShapeDtypeStruct((columns, size // 2, width), jnp.float32)
    sent = jax.ShapeDtypeStruct((2 * columns, size // 2, width), jnp.bfloat16)
    passed_on = jax.ShapeDtypeStruct((columns * size // 2 + depth, width), jnp.bfloat16)
    share = jax.ShapeDtypeStruct((depth, width), jnp.bfloat16)
    keep, up, down, ahead, behind = pl.pallas_call(
        products,
        out_shape=(full, sent, sent, waiting, pltpu.HBM(waiting.shape, waiting.dtype)),
        in_specs=[SMEM, VMEM, HBM],
        out_specs=(VMEM,) * 5,
        scratch_shapes=[
            pltpu.VMEM((col_blocks * size, total_rows), jnp.bfloat16),
            pltpu.SemaphoreType.DMA((columns,)),
        ],
        compiler_params=params,
        cost_estimate=pl.CostEstimate(flops=1700000000, bytes_accessed=9000000, transcendentals=0),
    )(place, received, pltpu.with_memory_space_constraint(turned, pltpu.HBM))
    up, down = passed(up, 1), passed(down, -1)
    ahead, behind, own = pl.pallas_call(
        relay,
        out_shape=(passed_on, passed_on, share),
        in_specs=[VMEM] * 5,
        out_specs=(VMEM,) * 3,
        compiler_params=params,
    )(terms, ahead, behind, up, down)
    ahead, behind, far = passed(ahead, 1), passed(behind, -1), passed(own, 2)
    share_spec = pl.BlockSpec((depth, width), lambda i: (0, 0))
    tail_spec = pl.BlockSpec((depth, width), lambda i: (columns * size // 2 // depth, 0))
    shares = pl.pallas_call(
        share_sum,
        grid=(1,),
        out_shape=jax.ShapeDtypeStruct((columns, depth, width), jnp.bfloat16),
        in_specs=[SMEM, share_spec, tail_spec, tail_spec, share_spec],
        out_specs=pl.BlockSpec((columns, depth, width), lambda i: (0, 0, 0)),
        scratch_shapes=[pltpu.VMEM((RING, depth, width), jnp.float32)],
        compiler_params=params,
    )(place, own, ahead, behind, far)
    own = jnp.sum(exchange(shares, "rep", axis_index_groups=groups).astype(jnp.float32), axis=0)
    parts = pl.pallas_call(
        add_ring,
        out_shape=jax.ShapeDtypeStruct((columns, size, width), jnp.bfloat16),
        in_specs=[VMEM] * 5,
        out_specs=VMEM,
        compiler_params=params,
    )(keep, up, down, ahead, behind)
    parts = exchange(parts, "rep", axis_index_groups=groups)

    own = own.astype(jnp.bfloat16)
    pair = jnp.concatenate([own, swapped(own, 1, "rows")], axis=0)
    others = [swapped(pair, mask, "rows") for mask in (2, 4, 6)]
    return pl.pallas_call(
        finish,
        out_shape=(
            jax.ShapeDtypeStruct((node_dev, width), jnp.bfloat16),
            jax.ShapeDtypeStruct((width, width), jnp.float32),
        ),
        in_specs=[SMEM] + [VMEM] * 6,
        out_specs=(VMEM, VMEM),
        compiler_params=params,
    )((lax.axis_index("rows") % SLICES).astype(jnp.int32)[None], parts, weight, pair, *others)


def solution(mesh):
    return jax.shard_map(
        per_device,
        mesh=mesh,
        in_specs=(
            P(("rows", "rep"), None),
            P(("rows", "rep"), None),
            P("rows", None),
            P(),
            P(("rows", "rep"), None, None),
            P(("rows", "rep"), None),
            P(("rows", "rep"), None),
            P(("rows", "rep")),
            P(("rows", "rep"), None, None, None),
        ),
        out_specs=(P(("rows", "rep"), None), P()),
        check_vma=False,
    )
```
